32 devices in a mesh: dp: 4 (over y, x), expert: 4 (over z), mp: 2 (over core).
Axes of the slice: x: 2, y: 2, z: 4, core: 2. Of those that a mesh axis runs over, the one named last changes fastest.
Arguments:
- tokens: float32 [2048, 1024], P(('dp', 'expert')), may hold values from -6 to 6
- block_experts: int32 [512, 1], P(('dp', 'expert')), may hold values from 0 to 3, as said below
- weight_up: bfloat16 [4, 1024, 2048], P('expert', None, 'mp'), may hold values from -0.1875 to 0.1875
- weight_down: bfloat16 [4, 2048, 1024], P('expert', 'mp'), may hold values from -0.125 to 0.125
- upstream: float32 [2048, 1024], P(('dp', 'expert')), may hold values from -6 to 6
Outputs:
- layer_output: float32 [2048, 1024], P(('dp', 'expert'))
- grad_tokens: float32 [2048, 1024], P(('dp', 'expert'))
- grad_up: float32 [4, 1024, 2048], P('expert', 'dp', 'mp')
- grad_down: float32 [4, 2048, 1024], P('expert', 'mp', 'dp')
The draws below stay inside these ranges and needn't reach their ends.
Inputs may be any that keep to these rules, and one draw needn't show every extreme that they name: `block_experts`: of the 32 cell blocks of one device, at most 16 name the same expert, and in every draw some expert is named by exactly 16 blocks of every device.
All inputs are finite; a program needn't handle non-finite values.
Results may differ from the reference program's by a relative error of at most 0.015.
Values may be sent and summed in bfloat16 or wider, within the bound.
A program may use at most 64 MiB of HBM per device.

```python
import jax
import jax.numpy as jnp
from jax import lax

D = 1024
FF = 2048
BLOCK = 4
EXPERTS = 4
BLOCKS_DEV = 32
CAP = 16
TOKENS = 2048
BLOCKS = 512
N_DP = 4
N_EXPERT = 4


def draw_block_experts(key, part):
    device_count = BLOCKS // BLOCKS_DEV
    slot_total = EXPERTS * CAP
    hot_count = max(1, BLOCKS_DEV // (4 * CAP))
    expert_rank = jax.random.permutation(jax.random.fold_in(key, 1), EXPERTS).astype(jnp.int32)
    slot_ids = jnp.arange(slot_total, dtype=jnp.int32)
    slot_rank = expert_rank[slot_ids // CAP]
    base_score = jnp.where(slot_rank < hot_count, 1 << 20, 0).astype(jnp.int32) + (EXPERTS - slot_rank)

    def draw_device(device_key):
        noise_draw = jax.random.randint(jax.random.fold_in(device_key, 2), (slot_total,), 0, EXPERTS, dtype=jnp.int32)
        score_all = (base_score + noise_draw) * slot_total + slot_ids
        top_vals, top_idx = lax.top_k(score_all, BLOCKS_DEV)
        chosen = (top_idx // CAP).astype(jnp.int32)
        shuffle = jax.random.permutation(jax.random.fold_in(device_key, 3), BLOCKS_DEV)
        return chosen[shuffle]
    device_keys = jax.random.split(jax.random.fold_in(key, 4), device_count)
    return jax.vmap(draw_device)(device_keys).reshape(BLOCKS, 1).astype(jnp.int32)


def spiked(entries, rng, source, target, blocks, factor):
    owner, partner = [(jnp.arange(entries.shape[axis_at]) // (entries.shape[axis_at] // blocks)).reshape([-1 if axis == axis_at else 1 for axis in range(entries.ndim)]) for axis_at in (source, target)]
    chosen = jax.random.permutation(rng, blocks)[partner]
    strong = (owner == chosen) | (owner == (partner + blocks // 2) % blocks)
    return jnp.where(strong, factor * entries, entries)


def level_of(key, dims, cuts, low, top_value):
    factor_of = 1.0
    for dim, parts in cuts:
        steps = jax.random.uniform(jax.random.fold_in(jax.random.fold_in(key, 6), dim), (parts,), jnp.float32, low / len(cuts), top_value / len(cuts))
        factor_of = factor_of * jnp.repeat(jnp.exp(steps), dims[dim] // parts).reshape((-1,) + (1,) * (len(dims) - 1 - dim))
    return factor_of


def noise(rng, extent, deviation, limit, shards=(), kind=jnp.bfloat16):
    entries = deviation * jax.random.normal(rng, extent, jnp.float32)
    if shards:
        entries = entries * level_of(rng, extent, shards, -0.22, 0.18)
    return jnp.clip(entries, -limit, limit).astype(kind)


def noise_with(rng, extent, spread, limit, shards, heavy, held_as=jnp.bfloat16):
    array = spread * jax.random.normal(rng, extent, jnp.float32)
    if shards:
        array = array * level_of(rng, extent, shards, -0.22, 0.18)
    return jnp.clip(spiked(array, jax.random.fold_in(rng, 3), *heavy), -limit, limit).astype(held_as)


def setup_inputs(seed: int = 0) -> dict:
    keys = jax.random.split(jax.random.key(seed), 6)
    return {
        "tokens": noise_with(keys[0], (TOKENS, D), 1.0, 6.0, ((0, 16),), (0, 1, 16, 2.0), jnp.float32),
        "block_experts": draw_block_experts(jax.random.fold_in(keys[5], 71), 0),
        "weight_up": noise(keys[2], (EXPERTS, D, FF), D ** -0.5, 0.1875, ((0, 4), (2, 2))),
        "weight_down": noise(keys[3], (EXPERTS, FF, D), FF ** -0.5, 0.125, ((0, 4), (1, 2))),
        "upstream": noise_with(keys[4], (TOKENS, D), 1.0, 6.0, ((0, 16),), (0, 1, 16, 2.0), jnp.float32),
    }


def reference(tokens, block_experts, weight_up, weight_down, upstream):
    groups = N_DP
    sources = N_EXPERT
    span = BLOCK * D
    tokens_lo = tokens.astype(jnp.bfloat16)
    upstream_lo = upstream.astype(jnp.bfloat16)
    token_blocks = tokens_lo.astype(jnp.float32).reshape(groups, sources, BLOCKS_DEV, span)
    upstream_blocks = upstream_lo.astype(jnp.float32).reshape(groups, sources, BLOCKS_DEV, span)
    labels = block_experts[:, 0].reshape(groups, sources, BLOCKS_DEV)
    matches = labels[..., :, None] == labels[..., None, :]
    order = jnp.arange(BLOCKS_DEV, dtype=jnp.int32)
    earlier = order[None, :] < order[:, None]
    block_rank = lax.optimization_barrier(jnp.sum(jnp.logical_and(matches, earlier).astype(jnp.int32), axis=-1))
    slot_index = jnp.arange(CAP, dtype=jnp.int32)
    row_count = sources * CAP * BLOCK

    def expert_step(carry, expert):
        output_acc, grad_acc = carry
        chosen = jnp.logical_and((labels == expert)[..., None], block_rank[..., None] == slot_index).astype(jnp.float32)
        routed_lo = jnp.einsum('gsbc,gsbk->gsck', chosen, token_blocks, precision=lax.Precision.HIGHEST)
        routed_lo = routed_lo.astype(jnp.bfloat16).reshape(groups * row_count, D)
        routed_up = jnp.einsum('gsbc,gsbk->gsck', chosen, upstream_blocks, precision=lax.Precision.HIGHEST)
        routed_up = routed_up.astype(jnp.bfloat16).reshape(groups * row_count, D)
        up_matrix = weight_up[expert]
        down_matrix = weight_down[expert]
        pre_act = jnp.dot(routed_lo, up_matrix, preferred_element_type=jnp.float32)
        hidden = jax.nn.gelu(pre_act).astype(jnp.bfloat16)
        mixed = jnp.dot(hidden, down_matrix, preferred_element_type=jnp.float32)
        hidden_grad = jnp.dot(routed_up, down_matrix.T, preferred_element_type=jnp.float32)
        unused, gelu_back = jax.vjp(jax.nn.gelu, pre_act)
        pre_grad = gelu_back(hidden_grad)[0].astype(jnp.bfloat16)
        token_grad = jnp.dot(pre_grad, up_matrix.T, preferred_element_type=jnp.float32)
        output_acc = output_acc + jnp.einsum('gsbc,gsck->gsbk', chosen, mixed.reshape(groups, sources, CAP, span), precision=lax.Precision.HIGHEST)
        grad_acc = grad_acc + jnp.einsum('gsbc,gsck->gsbk', chosen, token_grad.reshape(groups, sources, CAP, span), precision=lax.Precision.HIGHEST)
        up_part = jnp.einsum('grk,grf->gkf', routed_lo.reshape(groups, row_count, D).astype(jnp.float32), pre_grad.reshape(groups, row_count, FF).astype(jnp.float32))
        down_part = jnp.einsum('grf,grk->gfk', hidden.reshape(groups, row_count, FF).astype(jnp.float32), routed_up.reshape(groups, row_count, D).astype(jnp.float32))
        up_total = lax.optimization_barrier(jnp.sum(lax.optimization_barrier(up_part.astype(jnp.bfloat16)).astype(jnp.float32), axis=0))
        down_total = lax.optimization_barrier(jnp.sum(lax.optimization_barrier(down_part.astype(jnp.bfloat16)).astype(jnp.float32), axis=0))
        return ((output_acc, grad_acc), (up_total, down_total))
    zeros_init = jnp.zeros((groups, sources, BLOCKS_DEV, span), jnp.float32)
    finals, grads = lax.scan(expert_step, (zeros_init, zeros_init), jnp.arange(EXPERTS, dtype=jnp.int32))
    layer_output = tokens + finals[0].reshape(TOKENS, D)
    grad_tokens = upstream + finals[1].reshape(TOKENS, D)
    return (layer_output, grad_tokens, grads[0], grads[1])
```

```python
import jax
import jax.numpy as jnp
from jax import lax
from jax.experimental import pallas as pl
from jax.experimental.pallas import tpu as pltpu
from jax.sharding import PartitionSpec as P

MESH = pl.DeviceIdType.MESH
LAST = (((1,), (1,)), ((), ()))
FIRST = (((0,), (0,)), ((), ()))
F32 = jnp.float32
BF16 = jnp.bfloat16
TILE = 256


def flip(index, k):
    if k == 0:
        return index
    if k == 1:
        return index + 1 - 2 * lax.rem(index, 2)
    if k == 2:
        return lax.rem(index + 2, 4)
    return 3 - index


def remote(src, dst, send_sem, recv_sem, device):
    return pltpu.make_async_remote_copy(
        src_ref=src, dst_ref=dst, send_sem=send_sem, recv_sem=recv_sem, device_id=device, device_id_type=MESH
    )


def kernel(
    labels,
    tokens_hbm,
    upstream_hbm,
    up_hbm,
    down_hbm,
    home_out,
    grad_up_out,
    grad_down_out,
    rows_in,
    up,
    down,
    routed,
    gathered,
    hidden,
    pre_grad,
    parts,
    parts_in,
    summed,
    returned,
    mine,
    grad_up,
    grad_down,
    load_sem,
    store_sem,
    z_send,
    z_recv,
    x_send,
    x_recv,
    y_send,
    y_recv,
    s_send,
    s_recv,
    p_send,
    p_recv,
    r_send,
    r_recv,
    m_send,
    m_recv,
):
    dp = lax.axis_index("dp")
    me = lax.axis_index("expert")
    core = lax.axis_index("mp")
    other = 1 - core
    tok_rows, width = rows_in.shape[1], rows_in.shape[2]
    blocks_dev = labels.shape[0]
    block = tok_rows // blocks_dev
    slots = routed.shape[0]
    group = slots // 4
    share = grad_up.shape[0]
    units = up.shape[1]

    loads = [
        pltpu.make_async_copy(tokens_hbm, rows_in.at[0], load_sem.at[0]),
        pltpu.make_async_copy(upstream_hbm, rows_in.at[1], load_sem.at[1]),
        pltpu.make_async_copy(up_hbm, up, load_sem.at[2]),
        pltpu.make_async_copy(down_hbm, down, load_sem.at[3]),
    ]
    for load in loads:
        load.start()

    x_peer = {"dp": flip(dp, 1)}
    y_peer = {"dp": flip(dp, 2)}
    sibling = {"mp": other}
    z_peers = [{"expert": flip(me, k)} for k in range(4)]
    barrier = pltpu.get_barrier_semaphore()
    for peer in z_peers[1:] + [x_peer, y_peer, sibling]:
        pl.semaphore_signal(barrier, inc=1, device_id=peer, device_id_type=MESH)

    experts_at = lax.broadcasted_iota(jnp.int32, (blocks_dev, 128), 1)
    named = (labels[...] == experts_at).astype(F32)
    row_at = lax.broadcasted_iota(jnp.int32, (tok_rows, blocks_dev), 0)
    first_row = lax.broadcasted_iota(jnp.int32, (tok_rows, blocks_dev), 1) * block
    in_block = jnp.logical_and(row_at >= first_row, row_at < first_row + block)
    before = row_at >= first_row + block
    row_expert = jnp.dot(in_block.astype(F32), named, preferred_element_type=F32)
    row_rank = jnp.dot(before.astype(F32), named, preferred_element_type=F32)
    start = lax.broadcasted_iota(jnp.int32, (tok_rows, 128), 1).astype(F32) * group
    slot_of_row = jnp.sum(row_expert * (start + block * row_rank), axis=1, keepdims=True)
    slot_of_row += jnp.sum(jnp.where(in_block, row_at - first_row, 0).astype(F32), axis=1, keepdims=True)
    slot_at = lax.broadcasted_iota(jnp.int32, (tok_rows, slots), 1).astype(F32)
    picks = (slot_of_row == slot_at).astype(BF16)

    def rows_of(index):
        return pl.ds(pl.multiple_of(index * group, group), group)

    loads[0].wait()
    loads[1].wait()
    chosen = rows_in[core].astype(BF16)
    routed[...] = lax.dot_general(picks, chosen, FIRST, preferred_element_type=F32).astype(BF16)
    pl.semaphore_wait(barrier, 6)

    sent = []
    for k in (3, 2, 1):
        copy = remote(
            routed.at[rows_of(flip(me, k))],
            gathered.at[core, dp, rows_of(me)],
            z_send.at[k],
            z_recv.at[k],
            z_peers[k],
        )
        copy.start()
        sent.append(copy)
    gathered[core, dp, rows_of(me), :] = routed[rows_of(me), :]

    def push(which, array, rel, k, send, recv, index, peer):
        piece = gathered.at[array, flip(dp, rel), rows_of(flip(me, k))]
        copy = remote(piece, piece, send.at[index], recv.at[index], peer)
        if which == "start":
            copy.start()
            sent.append(copy)
        else:
            copy.wait_recv()

    def to_sibling(rel, k):
        push("start", core, rel, k, s_send, s_recv, rel * 4 + k, sibling)

    def from_sibling(rel):
        for k in range(4):
            push("wait", other, rel, k, s_send, s_recv, rel * 4 + k, sibling)

    def own_piece(k):
        if k:
            piece = gathered.at[core, dp, rows_of(flip(me, k))]
            remote(piece, piece, z_send.at[k], z_recv.at[k], z_peers[k]).wait_recv()
        push("start", core, 0, k, x_send, x_recv, k, x_peer)
        push("start", core, 0, k, y_send, y_recv, k, y_peer)
        to_sibling(0, k)

    def passed_piece(k):
        push("wait", core, 1, k, x_send, x_recv, k, x_peer)
        if k < 2:
            push("start", core, 1, k, y_send, y_recv, 4 + k, y_peer)
        to_sibling(1, k)
        push("wait", core, 2, k, y_send, y_recv, k, y_peer)
        if k >= 2:
            push("start", core, 2, k, x_send, x_recv, 2 + k, x_peer)
        to_sibling(2, k)

    def far_pieces():
        for k in range(4):
            if k < 2:
                push("wait", core, 3, k, y_send, y_recv, 4 + k, y_peer)
            else:
                push("wait", core, 3, k, x_send, x_recv, 2 + k, x_peer)
            to_sibling(3, k)

    mine_cols = pl.ds(pl.multiple_of(dp * share, share), share)

    def work(rel):
        at = flip(dp, rel)

        def step(index, carry):
            cols = pl.ds(pl.multiple_of(index * TILE, TILE), TILE)
            value = jnp.dot(gathered[0, at], up[:, cols], preferred_element_type=F32)
            back = lax.dot_general(gathered[1, at], down[cols, :], LAST, preferred_element_type=F32)
            square = value * value
            scale = 0.7978845608028654
            turn = jnp.tanh(scale * value * (1.0 + 0.044715 * square))
            cdf = 0.5 * (1.0 + turn)
            slope = cdf + (0.5 * scale) * value * (1.0 - turn * turn) * (1.0 + (3 * 0.044715) * square)
            hidden_lo = (value * cdf).astype(BF16)
            grad_lo = (back * slope).astype(BF16)
            part_up = lax.dot_general(gathered[0, at, :, mine_cols], grad_lo, FIRST, preferred_element_type=F32)
            part_down = lax.dot_general(hidden_lo, gathered[1, at, :, mine_cols], FIRST, preferred_element_type=F32)
            if rel == 0:
                hidden[:, cols] = hidden_lo
                pre_grad[:, cols] = grad_lo
                grad_up[:, cols] = part_up
                grad_down[cols, :] = part_down
            else:
                grad_up[:, cols] += part_up
                grad_down[cols, :] += part_down
            return carry

        lax.fori_loop(0, units // TILE, step, 0)

    own_piece(0)
    for k in range(1, 4):
        own_piece(k)
        passed_piece(k - 1)
    from_sibling(0)
    loads[2].wait()
    loads[3].wait()
    work(0)

    def out_step(index, carry):
        cols = pl.ds(pl.multiple_of(index * TILE, TILE), TILE)
        parts[0, :, cols] = jnp.dot(hidden[...], down[:, cols], preferred_element_type=F32).astype(BF16)
        parts[1, :, cols] = lax.dot_general(
            pre_grad[...], up[cols, :], LAST, preferred_element_type=F32
        ).astype(BF16)
        return carry

    lax.fori_loop(0, width // TILE, out_step, 0)
    swap = remote(parts.at[other], parts_in, p_send.at[0], p_recv.at[0], sibling)
    swap.start()
    sent.append(swap)
    passed_piece(3)
    swap.wait_recv()
    summed[...] = (parts[core].astype(F32) + parts_in[...].astype(F32)).astype(BF16)
    for k in (3, 2, 1):
        copy = remote(
            summed.at[rows_of(flip(me, k))],
            returned.at[rows_of(me)],
            r_send.at[k],
            r_recv.at[k],
            z_peers[k],
        )
        copy.start()
        sent.append(copy)
    returned[rows_of(me), :] = summed[rows_of(me), :]

    from_sibling(1)
    work(1)
    far_pieces()
    from_sibling(2)
    work(2)
    from_sibling(3)
    work(3)
    stores = [
        pltpu.make_async_copy(grad_up, grad_up_out, store_sem.at[0]),
        pltpu.make_async_copy(grad_down, grad_down_out, store_sem.at[1]),
    ]
    for store in stores:
        store.start()

    for k in (1, 2, 3):
        piece = returned.at[rows_of(flip(me, k))]
        remote(piece, piece, r_send.at[k], r_recv.at[k], z_peers[k]).wait_recv()
    mine[core] = jnp.dot(picks, returned[...], preferred_element_type=F32).astype(BF16)
    give = remote(mine.at[core], mine.at[core], m_send.at[0], m_recv.at[0], sibling)
    give.start()
    sent.append(give)
    remote(mine.at[other], mine.at[other], m_send.at[0], m_recv.at[0], sibling).wait_recv()
    final = pltpu.make_async_copy(mine, home_out, store_sem.at[2])
    final.start()
    for copy in sent:
        copy.wait_send()
    for store in stores + [final]:
        store.wait()


def fused_body(tokens, block_experts, weight_up, weight_down, upstream):
    tok_rows, width = tokens.shape
    blocks_dev = block_experts.shape[0]
    units = weight_up.shape[2]
    slots = 2 * tok_rows
    share = width // 4
    anywhere = pl.BlockSpec(memory_space=pl.ANY)
    flops = 2 * slots * width * units * 12
    home, grad_up, grad_down = pl.pallas_call(
        kernel,
        out_shape=(
            jax.ShapeDtypeStruct((2, tok_rows, width), BF16),
            jax.ShapeDtypeStruct((share, units), F32),
            jax.ShapeDtypeStruct((units, share), F32),
        ),
        in_specs=[pl.BlockSpec(memory_space=pltpu.VMEM)] + [anywhere] * 4,
        out_specs=(anywhere,) * 3,
        scratch_shapes=[
            pltpu.VMEM((2, tok_rows, width), F32),
            pltpu.VMEM((width, units), BF16),
            pltpu.VMEM((units, width), BF16),
            pltpu.VMEM((slots, width), BF16),
            pltpu.VMEM((2, 4, slots, width), BF16),
            pltpu.VMEM((slots, units), BF16),
            pltpu.VMEM((slots, units), BF16),
            pltpu.VMEM((2, slots, width), BF16),
            pltpu.VMEM((slots, width), BF16),
            pltpu.VMEM((slots, width), BF16),
            pltpu.VMEM((slots, width), BF16),
            pltpu.VMEM((2, tok_rows, width), BF16),
            pltpu.VMEM((share, units), F32),
            pltpu.VMEM((units, share), F32),
            pltpu.SemaphoreType.DMA((4,)),
            pltpu.SemaphoreType.DMA((3,)),
            pltpu.SemaphoreType.DMA((4,)),
            pltpu.SemaphoreType.DMA((4,)),
            pltpu.SemaphoreType.DMA((6,)),
            pltpu.SemaphoreType.DMA((6,)),
            pltpu.SemaphoreType.DMA((6,)),
            pltpu.SemaphoreType.DMA((6,)),
            pltpu.SemaphoreType.DMA((16,)),
            pltpu.SemaphoreType.DMA((16,)),
            pltpu.SemaphoreType.DMA((1,)),
            pltpu.SemaphoreType.DMA((1,)),
            pltpu.SemaphoreType.DMA((4,)),
            pltpu.SemaphoreType.DMA((4,)),
            pltpu.SemaphoreType.DMA((1,)),
            pltpu.SemaphoreType.DMA((1,)),
        ],
        compiler_params=pltpu.CompilerParams(
            collective_id=0, has_side_effects=True, vmem_limit_bytes=40 * 1024 * 1024
        ),
        cost_estimate=pl.CostEstimate(flops=flops, bytes_accessed=8 << 20, transcendentals=slots * units * 4),
    )(block_experts, tokens, upstream, weight_up[0], weight_down[0])
    return (
        tokens + home[0].astype(F32),
        upstream + home[1].astype(F32),
        grad_up[None],
        grad_down[None],
    )


def plain_body(tokens, block_experts, weight_up, weight_down, upstream):
    experts = lax.axis_size("expert")
    blocks_dev = block_experts.shape[0]
    tok_rows = tokens.shape[0]
    width = tokens.shape[1]
    block = tok_rows // blocks_dev
    capacity = max(1, blocks_dev * 2 // experts)
    slot_total = experts * capacity
    labels = block_experts[:, 0]
    order = jnp.arange(blocks_dev, dtype=jnp.int32)
    earlier = order[None, :] < order[:, None]
    matches = labels[:, None] == labels[None, :]
    block_rank = jnp.sum(jnp.logical_and(matches, earlier).astype(jnp.int32), axis=1)
    slot_of_block = labels * capacity + block_rank
    slot_match = slot_of_block[None, :] == jnp.arange(slot_total, dtype=jnp.int32)[:, None]
    source_block = jnp.sum(jnp.where(slot_match, order[None, :], 0), axis=1)
    occupied = jnp.any(slot_match, axis=1)

    def dispatch(rows_lo):
        blocks = rows_lo.reshape(blocks_dev, block, width)
        picked = jnp.take(blocks, source_block, axis=0)
        filled = jnp.where(occupied[:, None, None], picked, jnp.zeros((), rows_lo.dtype))
        outgoing = filled.reshape(experts, capacity * block, width)
        arrived = lax.all_to_all(outgoing, "expert", split_axis=0, concat_axis=0, tiled=True)
        return arrived.reshape(-1, width)

    def bring_home(partial_value):
        shaped = partial_value.reshape(experts, capacity * block, width)
        returned = lax.all_to_all(
            shaped.astype(jnp.bfloat16), "expert", split_axis=0, concat_axis=0, tiled=True
        ).astype(shaped.dtype)
        mine = jnp.take(returned.reshape(slot_total, block, width), slot_of_block, axis=0)
        result = lax.psum(mine.reshape(tok_rows, width).astype(jnp.bfloat16), "mp").astype(
            jnp.float32
        )
        return result

    up_matrix = weight_up[0]
    down_matrix = weight_down[0]
    contract_last = (((1,), (1,)), ((), ()))
    contract_first = (((0,), (0,)), ((), ()))
    routed_lo = dispatch(tokens.astype(jnp.bfloat16))
    pre_act = jnp.dot(routed_lo, up_matrix, preferred_element_type=jnp.float32)
    hidden = jax.nn.gelu(pre_act).astype(jnp.bfloat16)
    mixed_part = jnp.dot(hidden, down_matrix, preferred_element_type=jnp.float32)
    layer_output = tokens + bring_home(mixed_part)
    routed_up = dispatch(upstream.astype(jnp.bfloat16))
    hidden_grad = lax.dot_general(
        routed_up, down_matrix, contract_last, preferred_element_type=jnp.float32
    )
    unused, gelu_back = jax.vjp(jax.nn.gelu, pre_act)
    pre_grad = gelu_back(hidden_grad)[0].astype(jnp.bfloat16)
    token_part = lax.dot_general(
        pre_grad, up_matrix, contract_last, preferred_element_type=jnp.float32
    )
    up_part = lax.dot_general(
        routed_lo, pre_grad, contract_first, preferred_element_type=jnp.float32
    )
    down_part = lax.dot_general(
        hidden, routed_up, contract_first, preferred_element_type=jnp.float32
    )
    grad_tokens = upstream + bring_home(token_part)
    grad_up, grad_down = (
        lax.psum_scatter(
            up_part[None].astype(jnp.bfloat16), "dp", scatter_dimension=1, tiled=True
        ).astype(jnp.float32),
        lax.psum_scatter(
            down_part[None].astype(jnp.bfloat16), "dp", scatter_dimension=2, tiled=True
        ).astype(jnp.float32),
    )
    return (layer_output, grad_tokens, grad_up, grad_down)


def solution(mesh):
    placed = (
        P(("dp", "expert"), None),
        P(("dp", "expert"), None),
        P("expert", None, "mp"),
        P("expert", "mp", None),
        P(("dp", "expert"), None),
    )

    def body(tokens, block_experts, weight_up, weight_down, upstream):
        tok_rows, width = tokens.shape
        blocks_dev = block_experts.shape[0]
        fits = (
            (mesh.shape["dp"], mesh.shape["expert"], mesh.shape["mp"]) == (4, 4, 2)
            and blocks_dev % 2 == 0
            and (tok_rows // 2) % 16 == 0
            and width % (4 * TILE) == 0
            and weight_up.shape[2] % TILE == 0
        )
        chosen = fused_body if fits else plain_body
        return chosen(tokens, block_experts, weight_up, weight_down, upstream)

    return jax.shard_map(
        body,
        mesh=mesh,
        in_specs=placed,
        out_specs=(
            P(("dp", "expert"), None),
            P(("dp", "expert"), None),
            P("expert", "dp", "mp"),
            P("expert", "mp", "dp"),
        ),
        check_vma=False,
    )
```

```python
import jax
import jax.numpy as jnp
from jax import lax
from jax.experimental import pallas as pl
from jax.experimental.pallas import tpu as pltpu
from jax.sharding import PartitionSpec as P

MESH = pl.DeviceIdType.MESH
LAST = (((1,), (1,)), ((), ()))
FIRST = (((0,), (0,)), ((), ()))
F32 = jnp.float32
BF16 = jnp.bfloat16
TILE = 256


def flip(index, k):
    if k == 0:
        return index
    if k == 1:
        return index + 1 - 2 * lax.rem(index, 2)
    if k == 2:
        return lax.rem(index + 2, 4)
    return 3 - index


def remote(src, dst, send_sem, recv_sem, device):
    return pltpu.make_async_remote_copy(
        src_ref=src, dst_ref=dst, send_sem=send_sem, recv_sem=recv_sem, device_id=device, device_id_type=MESH
    )


def finish(first, second, third, fourth, first_out, second_out, third_out, fourth_out, sem):
    pairs = ((first, first_out), (second, second_out), (third, third_out), (fourth, fourth_out))
    copies = []
    for index, (src, dst) in enumerate(pairs):
        half = src.shape[0] // 2
        for part in range(2):
            rows = pl.ds(part * half, half)
            copies.append(pltpu.make_async_copy(src.at[rows], dst.at[rows], sem.at[2 * index + part]))
    for copy in copies:
        copy.start()
    for copy in copies:
        copy.wait()


def kernel(
    labels,
    tokens_hbm,
    upstream_hbm,
    up_hbm,
    down_hbm,
    layer_out,
    grad_tokens_out,
    grad_up_out,
    grad_down_out,
    rows_in,
    up,
    down,
    routed,
    gathered,
    hidden,
    slope_kept,
    pre_grad,
    parts,
    parts_in,
    summed,
    returned,
    grad_up,
    grad_down,
    load_sem,
    store_sem,
    z_send,
    z_recv,
    x_send,
    x_recv,
    y_send,
    y_recv,
    s_send,
    s_recv,
    p_send,
    p_recv,
    r_send,
    r_recv,
    h_send,
    h_recv,
):
    dp = lax.axis_index("dp")
    me = lax.axis_index("expert")
    core = lax.axis_index("mp")
    other = 1 - core
    tok_rows, width = rows_in.shape[1], rows_in.shape[2]
    blocks_dev = labels.shape[1]
    block = tok_rows // blocks_dev
    slots = routed.shape[1]
    half = slots // 2
    piece = half // 4
    share = grad_up.shape[0]
    units = up.shape[1]

    loads = [
        pltpu.make_async_copy(tokens_hbm, rows_in.at[0], load_sem.at[0]),
        pltpu.make_async_copy(upstream_hbm, rows_in.at[1], load_sem.at[1]),
        pltpu.make_async_copy(up_hbm, up, load_sem.at[2]),
        pltpu.make_async_copy(down_hbm, down, load_sem.at[3]),
    ]
    for load in loads:
        load.start()

    x_peer = {"dp": flip(dp, 1)}
    y_peer = {"dp": flip(dp, 2)}
    sibling = {"mp": other}
    z_peers = [{"expert": flip(me, k)} for k in range(4)]
    barrier = pltpu.get_barrier_semaphore()
    for peer in z_peers[1:] + [x_peer, y_peer, sibling]:
        pl.semaphore_signal(barrier, inc=1, device_id=peer, device_id_type=MESH)

    experts_at = lax.broadcasted_iota(jnp.int32, (128, blocks_dev), 0)
    named = (labels[...] == experts_at).astype(F32)
    row_at = lax.broadcasted_iota(jnp.int32, (tok_rows, blocks_dev), 0)
    first_row = lax.broadcasted_iota(jnp.int32, (tok_rows, blocks_dev), 1) * block
    in_block = jnp.logical_and(row_at >= first_row, row_at < first_row + block)
    before = row_at >= first_row + block
    row_expert = lax.dot_general(in_block.astype(F32), named, LAST, preferred_element_type=F32)
    row_rank = lax.dot_general(before.astype(F32), named, LAST, preferred_element_type=F32)
    start = lax.broadcasted_iota(jnp.int32, (tok_rows, 128), 1).astype(F32) * piece
    first_slot = jnp.sum(row_expert * start, axis=1, keepdims=True)
    place = jnp.sum(row_expert * (block * row_rank), axis=1, keepdims=True)
    place += jnp.sum(jnp.where(in_block, row_at - first_row, 0).astype(F32), axis=1, keepdims=True)
    slot_of_row = first_slot + place + jnp.where(place >= piece, float(half - piece), 0.0)
    slot_at = lax.broadcasted_iota(jnp.int32, (tok_rows, slots), 1).astype(F32)
    picks = (slot_of_row == slot_at).astype(BF16)

    def one(side, k):
        return pl.ds(pl.multiple_of(side * half + flip(me, k) * piece, piece), piece)

    def pair(side, p):
        q = lax.div(me, 2)
        at = q if p == 0 else 1 - q
        return pl.ds(pl.multiple_of(side * half + at * (2 * piece), 2 * piece), 2 * piece)

    sent = []

    def go(src, dst, send_sem, recv_sem, peer):
        copy = remote(src, dst, send_sem, recv_sem, peer)
        copy.start()
        sent.append(copy)

    def arrived(dst, send_sem, recv_sem, peer):
        remote(dst, dst, send_sem, recv_sem, peer).wait_recv()

    def route(a):
        loads[a].wait()
        rows_lo = rows_in[a].astype(BF16)
        routed[a] = lax.dot_general(picks, rows_lo, FIRST, preferred_element_type=F32).astype(BF16)

    def dispatch(a):
        for k in (2, 3, 1):
            go(
                routed.at[a, one(core, k)],
                gathered.at[a, dp, one(core, 0)],
                z_send.at[a, k],
                z_recv.at[a, k],
                z_peers[k],
            )
        gathered[a, dp, one(core, 0), :] = routed[a, one(core, 0), :]

    def block_at(a, rel, p, side=None):
        return gathered.at[a, flip(dp, rel), pair(core if side is None else side, p)]

    def to_sibling(a, rel, p):
        go(block_at(a, rel, p), block_at(a, rel, p), s_send.at[a, rel, p], s_recv.at[a, rel, p], sibling)

    def from_sibling(a, rel):
        for p in range(2):
            arrived(block_at(a, rel, p, other), s_send.at[a, rel, p], s_recv.at[a, rel, p], sibling)

    def spread(a, p):
        for k in (2 * p, 2 * p + 1):
            if k:
                arrived(gathered.at[a, dp, one(core, k)], z_send.at[a, k], z_recv.at[a, k], z_peers[k])
        to_sibling(a, 0, p)
        go(block_at(a, 0, p), block_at(a, 0, p), x_send.at[a, p], x_recv.at[a, p], x_peer)
        go(block_at(a, 0, p), block_at(a, 0, p), y_send.at[a, p], y_recv.at[a, p], y_peer)

    def pass_on(a, p):
        arrived(block_at(a, 1, p), x_send.at[a, p], x_recv.at[a, p], x_peer)
        if p == 0:
            go(block_at(a, 1, 0), block_at(a, 1, 0), y_send.at[a, 2], y_recv.at[a, 2], y_peer)
        to_sibling(a, 1, p)
        arrived(block_at(a, 2, p), y_send.at[a, p], y_recv.at[a, p], y_peer)
        if p == 1:
            go(block_at(a, 2, 1), block_at(a, 2, 1), x_send.at[a, 2], x_recv.at[a, 2], x_peer)
        to_sibling(a, 2, p)

    def from_corner(a):
        arrived(block_at(a, 3, 0), y_send.at[a, 2], y_recv.at[a, 2], y_peer)
        to_sibling(a, 3, 0)
        arrived(block_at(a, 3, 1), x_send.at[a, 2], x_recv.at[a, 2], x_peer)
        to_sibling(a, 3, 1)

    mine_cols = pl.ds(pl.multiple_of(dp * share, share), share)

    def activation(value):
        scale = 0.7978845608028654
        square = value * value
        turn = jnp.tanh(value * (scale + (scale * 0.044715) * square))
        cdf = 0.5 + 0.5 * turn
        slope = cdf + value * (0.5 - 0.5 * turn * turn) * (scale + (3 * scale * 0.044715) * square)
        return (value * cdf).astype(BF16), slope

    def tiles(total, step):
        def run(index, carry):
            step(pl.ds(pl.multiple_of(index * TILE, TILE), TILE))
            return carry

        lax.fori_loop(0, total // TILE, run, 0)

    def forward(cols):
        value = jnp.dot(gathered[0, dp], up[:, cols], preferred_element_type=F32)
        hidden[:, cols], slope_kept[:, cols] = activation(value)

    def mix(cols):
        parts[0, :, cols] = jnp.dot(hidden[...], down[:, cols], preferred_element_type=F32).astype(BF16)

    def backward(cols):
        back = lax.dot_general(gathered[1, dp], down[cols, :], LAST, preferred_element_type=F32)
        pre_grad[:, cols] = (back * slope_kept[:, cols]).astype(BF16)

    def unmix(cols):
        parts[1, :, cols] = lax.dot_general(
            pre_grad[...], up[cols, :], LAST, preferred_element_type=F32
        ).astype(BF16)

    def own_grads(cols):
        grad_up[:, cols] = lax.dot_general(
            gathered[0, dp, :, mine_cols], pre_grad[:, cols], FIRST, preferred_element_type=F32
        )
        grad_down[cols, :] = lax.dot_general(
            hidden[:, cols], gathered[1, dp, :, mine_cols], FIRST, preferred_element_type=F32
        )

    def other_grads(rel):
        at = flip(dp, rel)

        def step(cols):
            value = jnp.dot(gathered[0, at], up[:, cols], preferred_element_type=F32)
            back = lax.dot_general(gathered[1, at], down[cols, :], LAST, preferred_element_type=F32)
            hidden_lo, slope = activation(value)
            grad_lo = (back * slope).astype(BF16)
            grad_up[:, cols] += lax.dot_general(
                gathered[0, at, :, mine_cols], grad_lo, FIRST, preferred_element_type=F32
            )
            grad_down[cols, :] += lax.dot_general(
                hidden_lo, gathered[1, at, :, mine_cols], FIRST, preferred_element_type=F32
            )

        tiles(units, step)

    def swap(a):
        theirs = pl.ds(pl.multiple_of(other * half, half), half)
        go(parts.at[a, theirs], parts_in.at[a], p_send.at[a], p_recv.at[a], sibling)

    def send_home(a):
        arrived(parts_in.at[a], p_send.at[a], p_recv.at[a], sibling)
        ours = pl.ds(pl.multiple_of(core * half, half), half)
        summed[a] = (parts[a, ours, :].astype(F32) + parts_in[a].astype(F32)).astype(BF16)
        for k in (2, 3, 1):
            go(
                summed.at[a, pl.ds(pl.multiple_of(flip(me, k) * piece, piece), piece)],
                returned.at[a, one(core, 0)],
                r_send.at[a, k],
                r_recv.at[a, k],
                z_peers[k],
            )
        returned[a, one(core, 0), :] = summed[a, pl.ds(pl.multiple_of(me * piece, piece), piece), :]

    def reach_home(a, p):
        for k in (2 * p, 2 * p + 1):
            if k:
                arrived(returned.at[a, one(core, k)], r_send.at[a, k], r_recv.at[a, k], z_peers[k])
        block = returned.at[a, pair(core, p)]
        go(block, block, h_send.at[a, p], h_recv.at[a, p], sibling)

    stores = []

    def store(src, dst):
        copy = pltpu.make_async_copy(src, dst, store_sem.at[len(stores)])
        copy.start()
        stores.append(copy)

    def add_home(a, out):
        for p in range(2):
            arrived(returned.at[a, pair(other, p)], h_send.at[a, p], h_recv.at[a, p], sibling)
        rows_in[a] += jnp.dot(picks, returned[a], preferred_element_type=F32)
        store(rows_in.at[a], out)

    route(0)
    pl.semaphore_wait(barrier, 6)
    dispatch(0)
    route(1)
    spread(0, 0)
    dispatch(1)
    pass_on(0, 0)
    spread(0, 1)
    loads[2].wait()
    loads[3].wait()
    from_sibling(0, 0)
    tiles(units, forward)
    tiles(width, mix)
    swap(0)
    spread(1, 0)
    pass_on(0, 1)
    send_home(0)
    pass_on(1, 0)
    spread(1, 1)
    from_sibling(1, 0)
    tiles(units, backward)
    tiles(width, unmix)
    swap(1)
    from_corner(0)
    pass_on(1, 1)
    send_home(1)
    tiles(units, own_grads)
    for a in range(2):
        from_sibling(a, 1)
    other_grads(1)
    from_corner(1)
    for a in range(2):
        from_sibling(a, 2)
    other_grads(2)
    reach_home(0, 0)
    reach_home(0, 1)
    for a in range(2):
        from_sibling(a, 3)
    other_grads(3)
    store(grad_up, grad_up_out)
    store(grad_down, grad_down_out)
    reach_home(1, 0)
    add_home(0, layer_out)
    reach_home(1, 1)
    add_home(1, grad_tokens_out)
    for copy in sent:
        copy.wait_send()
    for copy in stores:
        copy.wait()


def fused_body(tokens, block_experts, weight_up, weight_down, upstream):
    tok_rows, width = tokens.shape
    blocks_dev = block_experts.shape[0]
    units = weight_up.shape[2]
    slots = 2 * tok_rows
    half = slots // 2
    share = width // 4
    in_hbm = pl.BlockSpec(memory_space=pltpu.HBM)
    anywhere = pl.BlockSpec(memory_space=pl.ANY)
    flops = 2 * slots * width * units * 12
    results = (
        jax.ShapeDtypeStruct((tok_rows, width), F32),
        jax.ShapeDtypeStruct((tok_rows, width), F32),
        jax.ShapeDtypeStruct((share, units), F32),
        jax.ShapeDtypeStruct((units, share), F32),
    )
    held = pl.pallas_call(
        kernel,
        out_shape=results,
        in_specs=[pl.BlockSpec(memory_space=pltpu.VMEM)] + [in_hbm] * 4,
        out_specs=(anywhere,) * 4,
        scratch_shapes=[
            pltpu.VMEM((2, tok_rows, width), F32),
            pltpu.VMEM((width, units), BF16),
            pltpu.VMEM((units, width), BF16),
            pltpu.VMEM((2, slots, width), BF16),
            pltpu.VMEM((2, 4, slots, width), BF16),
            pltpu.VMEM((slots, units), BF16),
            pltpu.VMEM((slots, units), F32),
            pltpu.VMEM((slots, units), BF16),
            pltpu.VMEM((2, slots, width), BF16),
            pltpu.VMEM((2, half, width), BF16),
            pltpu.VMEM((2, half, width), BF16),
            pltpu.VMEM((2, slots, width), BF16),
            pltpu.VMEM((share, units), F32),
            pltpu.VMEM((units, share), F32),
            pltpu.SemaphoreType.DMA((4,)),
            pltpu.SemaphoreType.DMA((4,)),
            pltpu.SemaphoreType.DMA((2, 4)),
            pltpu.SemaphoreType.DMA((2, 4)),
            pltpu.SemaphoreType.DMA((2, 3)),
            pltpu.SemaphoreType.DMA((2, 3)),
            pltpu.SemaphoreType.DMA((2, 3)),
            pltpu.SemaphoreType.DMA((2, 3)),
            pltpu.SemaphoreType.DMA((2, 4, 2)),
            pltpu.SemaphoreType.DMA((2, 4, 2)),
            pltpu.SemaphoreType.DMA((2,)),
            pltpu.SemaphoreType.DMA((2,)),
            pltpu.SemaphoreType.DMA((2, 4)),
            pltpu.SemaphoreType.DMA((2, 4)),
            pltpu.SemaphoreType.DMA((2, 2)),
            pltpu.SemaphoreType.DMA((2, 2)),
        ],
        compiler_params=pltpu.CompilerParams(
            collective_id=0, has_side_effects=True, vmem_limit_bytes=40 * 1024 * 1024
        ),
        cost_estimate=pl.CostEstimate(flops=flops, bytes_accessed=8 << 20, transcendentals=slots * units * 4),
    )(block_experts.reshape(1, blocks_dev), tokens, upstream, weight_up[0], weight_down[0])
    layer_output, grad_tokens, grad_up, grad_down = pl.pallas_call(
        finish,
        out_shape=results,
        in_specs=[anywhere] * 4,
        out_specs=(in_hbm,) * 4,
        scratch_shapes=[pltpu.SemaphoreType.DMA((8,))],
        cost_estimate=pl.CostEstimate(flops=0, bytes_accessed=3 << 20, transcendentals=0),
    )(*held)
    return layer_output, grad_tokens, grad_up[None], grad_down[None]


def plain_body(tokens, block_experts, weight_up, weight_down, upstream):
    experts = lax.axis_size("expert")
    blocks_dev = block_experts.shape[0]
    tok_rows = tokens.shape[0]
    width = tokens.shape[1]
    block = tok_rows // blocks_dev
    capacity = max(1, blocks_dev * 2 // experts)
    slot_total = experts * capacity
    labels = block_experts[:, 0]
    order = jnp.arange(blocks_dev, dtype=jnp.int32)
    earlier = order[None, :] < order[:, None]
    matches = labels[:, None] == labels[None, :]
    block_rank = jnp.sum(jnp.logical_and(matches, earlier).astype(jnp.int32), axis=1)
    slot_of_block = labels * capacity + block_rank
    slot_match = slot_of_block[None, :] == jnp.arange(slot_total, dtype=jnp.int32)[:, None]
    source_block = jnp.sum(jnp.where(slot_match, order[None, :], 0), axis=1)
    occupied = jnp.any(slot_match, axis=1)

    def dispatch(rows_lo):
        blocks = rows_lo.reshape(blocks_dev, block, width)
        picked = jnp.take(blocks, source_block, axis=0)
        filled = jnp.where(occupied[:, None, None], picked, jnp.zeros((), rows_lo.dtype))
        outgoing = filled.reshape(experts, capacity * block, width)
        arrived = lax.all_to_all(outgoing, "expert", split_axis=0, concat_axis=0, tiled=True)
        return arrived.reshape(-1, width)

    def bring_home(partial_value):
        shaped = partial_value.reshape(experts, capacity * block, width)
        returned = lax.all_to_all(
            shaped.astype(jnp.bfloat16), "expert", split_axis=0, concat_axis=0, tiled=True
        ).astype(shaped.dtype)
        mine = jnp.take(returned.reshape(slot_total, block, width), slot_of_block, axis=0)
        result = lax.psum(mine.reshape(tok_rows, width).astype(jnp.bfloat16), "mp").astype(
            jnp.float32
        )
        return result

    up_matrix = weight_up[0]
    down_matrix = weight_down[0]
    contract_last = (((1,), (1,)), ((), ()))
    contract_first = (((0,), (0,)), ((), ()))
    routed_lo = dispatch(tokens.astype(jnp.bfloat16))
    pre_act = jnp.dot(routed_lo, up_matrix, preferred_element_type=jnp.float32)
    hidden = jax.nn.gelu(pre_act).astype(jnp.bfloat16)
    mixed_part = jnp.dot(hidden, down_matrix, preferred_element_type=jnp.float32)
    layer_output = tokens + bring_home(mixed_part)
    routed_up = dispatch(upstream.astype(jnp.bfloat16))
    hidden_grad = lax.dot_general(
        routed_up, down_matrix, contract_last, preferred_element_type=jnp.float32
    )
    unused, gelu_back = jax.vjp(jax.nn.gelu, pre_act)
    pre_grad = gelu_back(hidden_grad)[0].astype(jnp.bfloat16)
    token_part = lax.dot_general(
        pre_grad, up_matrix, contract_last, preferred_element_type=jnp.float32
    )
    up_part = lax.dot_general(
        routed_lo, pre_grad, contract_first, preferred_element_type=jnp.float32
    )
    down_part = lax.dot_general(
        hidden, routed_up, contract_first, preferred_element_type=jnp.float32
    )
    grad_tokens = upstream + bring_home(token_part)
    grad_up, grad_down = (
        lax.psum_scatter(
            up_part[None].astype(jnp.bfloat16), "dp", scatter_dimension=1, tiled=True
        ).astype(jnp.float32),
        lax.psum_scatter(
            down_part[None].astype(jnp.bfloat16), "dp", scatter_dimension=2, tiled=True
        ).astype(jnp.float32),
    )
    return (layer_output, grad_tokens, grad_up, grad_down)


def solution(mesh):
    placed = (
        P(("dp", "expert"), None),
        P(("dp", "expert"), None),
        P("expert", None, "mp"),
        P("expert", "mp", None),
        P(("dp", "expert"), None),
    )

    def body(tokens, block_experts, weight_up, weight_down, upstream):
        tok_rows, width = tokens.shape
        blocks_dev = block_experts.shape[0]
        fits = (
            (mesh.shape["dp"], mesh.shape["expert"], mesh.shape["mp"]) == (4, 4, 2)
            and blocks_dev % 2 == 0
            and (tok_rows // 4) % 16 == 0
            and width % (4 * TILE) == 0
            and weight_up.shape[2] % TILE == 0
        )
        chosen = fused_body if fits else plain_body
        return chosen(tokens, block_experts, weight_up, weight_down, upstream)

    return jax.shard_map(
        body,
        mesh=mesh,
        in_specs=placed,
        out_specs=(
            P(("dp", "expert"), None),
            P(("dp", "expert"), None),
            P("expert", "dp", "mp"),
            P("expert", "mp", "dp"),
        ),
        check_vma=False,
    )
```

```python
import jax
import jax.numpy as jnp
from jax import lax
from jax.experimental import pallas as pl
from jax.experimental.pallas import tpu as pltpu
from jax.sharding import PartitionSpec as P

MESH = pl.DeviceIdType.MESH
LAST = (((1,), (1,)), ((), ()))
FIRST = (((0,), (0,)), ((), ()))
F32 = jnp.float32
BF16 = jnp.bfloat16
TILE = 256
GRANT = 57 * 1024 * 1024


def flip(index, k):
    if k == 0:
        return index
    if k == 1:
        return index + 1 - 2 * lax.rem(index, 2)
    if k == 2:
        return lax.rem(index + 2, 4)
    return 3 - index


def remote(src, dst, send_sem, recv_sem, device):
    return pltpu.make_async_remote_copy(
        src_ref=src, dst_ref=dst, send_sem=send_sem, recv_sem=recv_sem, device_id=device, device_id_type=MESH
    )


def finish(*refs):
    sources, results, held = refs[:4], refs[4:8], refs[8:12]
    in_sem, out_sem = refs[12:]
    loads, stores = [], []
    for src, dst, kept in zip(sources, results, held):
        half = src.shape[0] // 2
        for part in range(2):
            rows = pl.ds(part * half, half)
            index = len(loads)
            loads.append(pltpu.make_async_copy(src.at[rows], kept.at[rows], in_sem.at[index]))
            stores.append(pltpu.make_async_copy(kept.at[rows], dst.at[rows], out_sem.at[index]))
    for load in loads:
        load.start()
    for load, store in zip(loads, stores):
        load.wait()
        store.start()
    for store in stores:
        store.wait()


def kernel(
    labels,
    tokens_hbm,
    upstream_hbm,
    up_hbm,
    down_hbm,
    layer_out,
    grad_tokens_out,
    grad_up_out,
    grad_down_out,
    rows_in,
    up,
    down,
    routed,
    gathered,
    hidden,
    slope_kept,
    pre_grad,
    parts,
    parts_in,
    summed,
    returned,
    grad_up,
    grad_down,
    load_sem,
    store_sem,
    z_send,
    z_recv,
    x_send,
    x_recv,
    y_send,
    y_recv,
    s_send,
    s_recv,
    p_send,
    p_recv,
    r_send,
    r_recv,
    h_send,
    h_recv,
):
    dp = lax.axis_index("dp")
    me = lax.axis_index("expert")
    core = lax.axis_index("mp")
    other = 1 - core
    tok_rows, width = rows_in.shape[1], rows_in.shape[2]
    blocks_dev = labels.shape[1]
    block = tok_rows // blocks_dev
    slots = routed.shape[1]
    half = slots // 2
    piece = half // 4
    share = grad_up.shape[0]
    units = up.shape[1]

    loads = [
        pltpu.make_async_copy(tokens_hbm, rows_in.at[0], load_sem.at[0]),
        pltpu.make_async_copy(upstream_hbm, rows_in.at[1], load_sem.at[1]),
        pltpu.make_async_copy(up_hbm, up, load_sem.at[2]),
        pltpu.make_async_copy(down_hbm, down, load_sem.at[3]),
    ]
    for load in loads:
        load.start()

    x_peer = {"dp": flip(dp, 1)}
    y_peer = {"dp": flip(dp, 2)}
    sibling = {"mp": other}
    z_peers = [{"expert": flip(me, k)} for k in range(4)]
    barrier = pltpu.get_barrier_semaphore()
    for peer in z_peers[1:] + [x_peer, y_peer, sibling]:
        pl.semaphore_signal(barrier, inc=1, device_id=peer, device_id_type=MESH)

    experts_at = lax.broadcasted_iota(jnp.int32, (128, blocks_dev), 0)
    named = (labels[...] == experts_at).astype(F32)
    row_at = lax.broadcasted_iota(jnp.int32, (tok_rows, blocks_dev), 0)
    first_row = lax.broadcasted_iota(jnp.int32, (tok_rows, blocks_dev), 1) * block
    in_block = jnp.logical_and(row_at >= first_row, row_at < first_row + block)
    before = row_at >= first_row + block
    row_expert = lax.dot_general(in_block.astype(F32), named, LAST, preferred_element_type=F32)
    row_rank = lax.dot_general(before.astype(F32), named, LAST, preferred_element_type=F32)
    start = lax.broadcasted_iota(jnp.int32, (tok_rows, 128), 1).astype(F32) * piece
    first_slot = jnp.sum(row_expert * start, axis=1, keepdims=True)
    place = jnp.sum(row_expert * (block * row_rank), axis=1, keepdims=True)
    place += jnp.sum(jnp.where(in_block, row_at - first_row, 0).astype(F32), axis=1, keepdims=True)
    slot_of_row = first_slot + place + jnp.where(place >= piece, float(half - piece), 0.0)
    slot_at = lax.broadcasted_iota(jnp.int32, (tok_rows, slots), 1).astype(F32)
    picks = (slot_of_row == slot_at).astype(BF16)

    def one(side, k):
        return pl.ds(pl.multiple_of(side * half + flip(me, k) * piece, piece), piece)

    def pair(side, p):
        q = lax.div(me, 2)
        at = q if p == 0 else 1 - q
        return pl.ds(pl.multiple_of(side * half + at * (2 * piece), 2 * piece), 2 * piece)

    sent = []

    def go(src, dst, send_sem, recv_sem, peer):
        copy = remote(src, dst, send_sem, recv_sem, peer)
        copy.start()
        sent.append(copy)

    def arrived(dst, send_sem, recv_sem, peer):
        remote(dst, dst, send_sem, recv_sem, peer).wait_recv()

    def route(a):
        loads[a].wait()
        rows_lo = rows_in[a].astype(BF16)
        routed[a] = lax.dot_general(picks, rows_lo, FIRST, preferred_element_type=F32).astype(BF16)

    def dispatch(a):
        for k in (2, 3, 1):
            go(
                routed.at[a, one(core, k)],
                gathered.at[a, dp, one(core, 0)],
                z_send.at[a, k],
                z_recv.at[a, k],
                z_peers[k],
            )
        gathered[a, dp, one(core, 0), :] = routed[a, one(core, 0), :]

    def block_at(a, rel, p, side=None):
        return gathered.at[a, flip(dp, rel), pair(core if side is None else side, p)]

    def to_sibling(a, rel, p):
        go(block_at(a, rel, p), block_at(a, rel, p), s_send.at[a, rel, p], s_recv.at[a, rel, p], sibling)

    def from_sibling(a, rel):
        for p in range(2):
            arrived(block_at(a, rel, p, other), s_send.at[a, rel, p], s_recv.at[a, rel, p], sibling)

    def spread(a, p):
        for k in (2 * p, 2 * p + 1):
            if k:
                arrived(gathered.at[a, dp, one(core, k)], z_send.at[a, k], z_recv.at[a, k], z_peers[k])
        to_sibling(a, 0, p)
        go(block_at(a, 0, p), block_at(a, 0, p), x_send.at[a, p], x_recv.at[a, p], x_peer)
        go(block_at(a, 0, p), block_at(a, 0, p), y_send.at[a, p], y_recv.at[a, p], y_peer)

    def pass_on(a, p):
        arrived(block_at(a, 1, p), x_send.at[a, p], x_recv.at[a, p], x_peer)
        if p == 0:
            go(block_at(a, 1, 0), block_at(a, 1, 0), y_send.at[a, 2], y_recv.at[a, 2], y_peer)
        to_sibling(a, 1, p)
        arrived(block_at(a, 2, p), y_send.at[a, p], y_recv.at[a, p], y_peer)
        if p == 1:
            go(block_at(a, 2, 1), block_at(a, 2, 1), x_send.at[a, 2], x_recv.at[a, 2], x_peer)
        to_sibling(a, 2, p)

    def from_corner(a):
        arrived(block_at(a, 3, 0), y_send.at[a, 2], y_recv.at[a, 2], y_peer)
        to_sibling(a, 3, 0)
        arrived(block_at(a, 3, 1), x_send.at[a, 2], x_recv.at[a, 2], x_peer)
        to_sibling(a, 3, 1)

    mine_cols = pl.ds(pl.multiple_of(dp * share, share), share)

    def activation(value):
        scale = 0.7978845608028654
        square = value * value
        turn = jnp.tanh(value * (scale + (scale * 0.044715) * square))
        cdf = 0.5 + 0.5 * turn
        slope = cdf + value * (0.5 - 0.5 * turn * turn) * (scale + (3 * scale * 0.044715) * square)
        return (value * cdf).astype(BF16), slope

    def tiles(total, step):
        for index in range(total // TILE):
            step(pl.ds(index * TILE, TILE))

    def forward(cols):
        value = jnp.dot(gathered[0, dp], up[:, cols], preferred_element_type=F32)
        hidden[:, cols], slope_kept[:, cols] = activation(value)

    def mix(cols):
        parts[0, :, cols] = jnp.dot(hidden[...], down[:, cols], preferred_element_type=F32).astype(BF16)

    def backward(cols):
        back = lax.dot_general(gathered[1, dp], down[cols, :], LAST, preferred_element_type=F32)
        pre_grad[:, cols] = (back * slope_kept[:, cols]).astype(BF16)

    def unmix(cols):
        parts[1, :, cols] = lax.dot_general(
            pre_grad[...], up[cols, :], LAST, preferred_element_type=F32
        ).astype(BF16)

    def own_grads(cols):
        grad_up[:, cols] = lax.dot_general(
            gathered[0, dp, :, mine_cols], pre_grad[:, cols], FIRST, preferred_element_type=F32
        )
        grad_down[cols, :] = lax.dot_general(
            hidden[:, cols], gathered[1, dp, :, mine_cols], FIRST, preferred_element_type=F32
        )

    def other_grads(rel):
        at = flip(dp, rel)

        def step(cols):
            value = jnp.dot(gathered[0, at], up[:, cols], preferred_element_type=F32)
            back = lax.dot_general(gathered[1, at], down[cols, :], LAST, preferred_element_type=F32)
            hidden_lo, slope = activation(value)
            grad_lo = (back * slope).astype(BF16)
            grad_up[:, cols] += lax.dot_general(
                gathered[0, at, :, mine_cols], grad_lo, FIRST, preferred_element_type=F32
            )
            grad_down[cols, :] += lax.dot_general(
                hidden_lo, gathered[1, at, :, mine_cols], FIRST, preferred_element_type=F32
            )

        tiles(units, step)

    def swap(a):
        theirs = pl.ds(pl.multiple_of(other * half, half), half)
        go(parts.at[a, theirs], parts_in.at[a], p_send.at[a], p_recv.at[a], sibling)

    def send_home(a):
        arrived(parts_in.at[a], p_send.at[a], p_recv.at[a], sibling)
        ours = pl.ds(pl.multiple_of(core * half, half), half)
        summed[a] = (parts[a, ours, :].astype(F32) + parts_in[a].astype(F32)).astype(BF16)
        for k in (2, 3, 1):
            go(
                summed.at[a, pl.ds(pl.multiple_of(flip(me, k) * piece, piece), piece)],
                returned.at[a, one(core, 0)],
                r_send.at[a, k],
                r_recv.at[a, k],
                z_peers[k],
            )
        returned[a, one(core, 0), :] = summed[a, pl.ds(pl.multiple_of(me * piece, piece), piece), :]

    def reach_home(a, p):
        for k in (2 * p, 2 * p + 1):
            if k:
                arrived(returned.at[a, one(core, k)], r_send.at[a, k], r_recv.at[a, k], z_peers[k])
        block = returned.at[a, pair(core, p)]
        go(block, block, h_send.at[a, p], h_recv.at[a, p], sibling)

    stores = []

    def store(src, dst):
        copy = pltpu.make_async_copy(src, dst, store_sem.at[len(stores)])
        copy.start()
        stores.append(copy)

    def add_home(a, out):
        for p in range(2):
            arrived(returned.at[a, pair(other, p)], h_send.at[a, p], h_recv.at[a, p], sibling)
        rows_in[a] += jnp.dot(picks, returned[a], preferred_element_type=F32)
        store(rows_in.at[a], out)

    route(0)
    pl.semaphore_wait(barrier, 6)
    dispatch(0)
    route(1)
    spread(0, 0)
    dispatch(1)
    pass_on(0, 0)
    spread(0, 1)
    loads[2].wait()
    loads[3].wait()
    from_sibling(0, 0)
    tiles(units, forward)
    tiles(width, mix)
    swap(0)
    spread(1, 0)
    spread(1, 1)
    send_home(0)
    pass_on(0, 1)
    from_sibling(1, 0)
    tiles(units, backward)
    tiles(width, unmix)
    swap(1)
    pass_on(1, 0)
    tiles(units, own_grads)
    send_home(1)
    from_corner(0)
    pass_on(1, 1)
    for a in range(2):
        from_sibling(a, 1)
    other_grads(1)
    from_corner(1)
    for a in range(2):
        from_sibling(a, 2)
    other_grads(2)
    reach_home(0, 0)
    reach_home(0, 1)
    for a in range(2):
        from_sibling(a, 3)
    other_grads(3)
    store(grad_up, grad_up_out)
    store(grad_down, grad_down_out)
    reach_home(1, 0)
    add_home(0, layer_out)
    reach_home(1, 1)
    add_home(1, grad_tokens_out)
    for copy in sent:
        copy.wait_send()
    for copy in stores:
        copy.wait()


def fused_body(tokens, block_experts, weight_up, weight_down, upstream):
    tok_rows, width = tokens.shape
    blocks_dev = block_experts.shape[0]
    units = weight_up.shape[2]
    slots = 2 * tok_rows
    half = slots // 2
    share = width // 4
    in_hbm = pl.BlockSpec(memory_space=pltpu.HBM)
    anywhere = pl.BlockSpec(memory_space=pl.ANY)
    flops = 2 * slots * width * units * 12
    results = (
        jax.ShapeDtypeStruct((tok_rows, width), F32),
        jax.ShapeDtypeStruct((tok_rows, width), F32),
        jax.ShapeDtypeStruct((share, units), F32),
        jax.ShapeDtypeStruct((units, share), F32),
    )
    held = pl.pallas_call(
        kernel,
        out_shape=results,
        in_specs=[pl.BlockSpec(memory_space=pltpu.VMEM)] + [in_hbm] * 4,
        out_specs=(anywhere,) * 4,
        scratch_shapes=[
            pltpu.VMEM((2, tok_rows, width), F32),
            pltpu.VMEM((width, units), BF16),
            pltpu.VMEM((units, width), BF16),
            pltpu.VMEM((2, slots, width), BF16),
            pltpu.VMEM((2, 4, slots, width), BF16),
            pltpu.VMEM((slots, units), BF16),
            pltpu.VMEM((slots, units), F32),
            pltpu.VMEM((slots, units), BF16),
            pltpu.VMEM((2, slots, width), BF16),
            pltpu.VMEM((2, half, width), BF16),
            pltpu.VMEM((2, half, width), BF16),
            pltpu.VMEM((2, slots, width), BF16),
            pltpu.VMEM((share, units), F32),
            pltpu.VMEM((units, share), F32),
            pltpu.SemaphoreType.DMA((4,)),
            pltpu.SemaphoreType.DMA((4,)),
            pltpu.SemaphoreType.DMA((2, 4)),
            pltpu.SemaphoreType.DMA((2, 4)),
            pltpu.SemaphoreType.DMA((2, 3)),
            pltpu.SemaphoreType.DMA((2, 3)),
            pltpu.SemaphoreType.DMA((2, 3)),
            pltpu.SemaphoreType.DMA((2, 3)),
            pltpu.SemaphoreType.DMA((2, 4, 2)),
            pltpu.SemaphoreType.DMA((2, 4, 2)),
            pltpu.SemaphoreType.DMA((2,)),
            pltpu.SemaphoreType.DMA((2,)),
            pltpu.SemaphoreType.DMA((2, 4)),
            pltpu.SemaphoreType.DMA((2, 4)),
            pltpu.SemaphoreType.DMA((2, 2)),
            pltpu.SemaphoreType.DMA((2, 2)),
        ],
        compiler_params=pltpu.CompilerParams(
            collective_id=0, has_side_effects=True, vmem_limit_bytes=GRANT
        ),
        cost_estimate=pl.CostEstimate(flops=flops, bytes_accessed=8 << 20, transcendentals=slots * units * 4),
    )(block_experts.reshape(1, blocks_dev), tokens, upstream, weight_up[0], weight_down[0])
    layer_output, grad_tokens, grad_up, grad_down = pl.pallas_call(
        finish,
        out_shape=results,
        in_specs=[anywhere] * 4,
        out_specs=(in_hbm,) * 4,
        scratch_shapes=[pltpu.VMEM(result.shape, F32) for result in results]
        + [pltpu.SemaphoreType.DMA((8,)), pltpu.SemaphoreType.DMA((8,))],
        compiler_params=pltpu.CompilerParams(vmem_limit_bytes=GRANT),
        cost_estimate=pl.CostEstimate(flops=0, bytes_accessed=3 << 20, transcendentals=0),
    )(*held)
    return layer_output, grad_tokens, grad_up[None], grad_down[None]


def plain_body(tokens, block_experts, weight_up, weight_down, upstream):
    experts = lax.axis_size("expert")
    blocks_dev = block_experts.shape[0]
    tok_rows = tokens.shape[0]
    width = tokens.shape[1]
    block = tok_rows // blocks_dev
    capacity = max(1, blocks_dev * 2 // experts)
    slot_total = experts * capacity
    labels = block_experts[:, 0]
    order = jnp.arange(blocks_dev, dtype=jnp.int32)
    earlier = order[None, :] < order[:, None]
    matches = labels[:, None] == labels[None, :]
    block_rank = jnp.sum(jnp.logical_and(matches, earlier).astype(jnp.int32), axis=1)
    slot_of_block = labels * capacity + block_rank
    slot_match = slot_of_block[None, :] == jnp.arange(slot_total, dtype=jnp.int32)[:, None]
    source_block = jnp.sum(jnp.where(slot_match, order[None, :], 0), axis=1)
    occupied = jnp.any(slot_match, axis=1)

    def dispatch(rows_lo):
        blocks = rows_lo.reshape(blocks_dev, block, width)
        picked = jnp.take(blocks, source_block, axis=0)
        filled = jnp.where(occupied[:, None, None], picked, jnp.zeros((), rows_lo.dtype))
        outgoing = filled.reshape(experts, capacity * block, width)
        arrived = lax.all_to_all(outgoing, "expert", split_axis=0, concat_axis=0, tiled=True)
        return arrived.reshape(-1, width)

    def bring_home(partial_value):
        shaped = partial_value.reshape(experts, capacity * block, width)
        returned = lax.all_to_all(
            shaped.astype(jnp.bfloat16), "expert", split_axis=0, concat_axis=0, tiled=True
        ).astype(shaped.dtype)
        mine = jnp.take(returned.reshape(slot_total, block, width), slot_of_block, axis=0)
        result = lax.psum(mine.reshape(tok_rows, width).astype(jnp.bfloat16), "mp").astype(
            jnp.float32
        )
        return result

    up_matrix = weight_up[0]
    down_matrix = weight_down[0]
    contract_last = (((1,), (1,)), ((), ()))
    contract_first = (((0,), (0,)), ((), ()))
    routed_lo = dispatch(tokens.astype(jnp.bfloat16))
    pre_act = jnp.dot(routed_lo, up_matrix, preferred_element_type=jnp.float32)
    hidden = jax.nn.gelu(pre_act).astype(jnp.bfloat16)
    mixed_part = jnp.dot(hidden, down_matrix, preferred_element_type=jnp.float32)
    layer_output = tokens + bring_home(mixed_part)
    routed_up = dispatch(upstream.astype(jnp.bfloat16))
    hidden_grad = lax.dot_general(
        routed_up, down_matrix, contract_last, preferred_element_type=jnp.float32
    )
    unused, gelu_back = jax.vjp(jax.nn.gelu, pre_act)
    pre_grad = gelu_back(hidden_grad)[0].astype(jnp.bfloat16)
    token_part = lax.dot_general(
        pre_grad, up_matrix, contract_last, preferred_element_type=jnp.float32
    )
    up_part = lax.dot_general(
        routed_lo, pre_grad, contract_first, preferred_element_type=jnp.float32
    )
    down_part = lax.dot_general(
        hidden, routed_up, contract_first, preferred_element_type=jnp.float32
    )
    grad_tokens = upstream + bring_home(token_part)
    grad_up, grad_down = (
        lax.psum_scatter(
            up_part[None].astype(jnp.bfloat16), "dp", scatter_dimension=1, tiled=True
        ).astype(jnp.float32),
        lax.psum_scatter(
            down_part[None].astype(jnp.bfloat16), "dp", scatter_dimension=2, tiled=True
        ).astype(jnp.float32),
    )
    return (layer_output, grad_tokens, grad_up, grad_down)


def solution(mesh):
    placed = (
        P(("dp", "expert"), None),
        P(("dp", "expert"), None),
        P("expert", None, "mp"),
        P("expert", "mp", None),
        P(("dp", "expert"), None),
    )

    def body(tokens, block_experts, weight_up, weight_down, upstream):
        tok_rows, width = tokens.shape
        blocks_dev = block_experts.shape[0]
        fits = (
            (mesh.shape["dp"], mesh.shape["expert"], mesh.shape["mp"]) == (4, 4, 2)
            and blocks_dev % 2 == 0
            and (tok_rows // 4) % 16 == 0
            and width % (4 * TILE) == 0
            and weight_up.shape[2] % TILE == 0
        )
        chosen = fused_body if fits else plain_body
        return chosen(tokens, block_experts, weight_up, weight_down, upstream)

    return jax.shard_map(
        body,
        mesh=mesh,
        in_specs=placed,
        out_specs=(
            P(("dp", "expert"), None),
            P(("dp", "expert"), None),
            P("expert", "dp", "mp"),
            P("expert", "mp", "dp"),
        ),
        check_vma=False,
    )
```

```python
import jax
import jax.numpy as jnp
from jax import lax
from jax.experimental import pallas as pl
from jax.experimental.pallas import tpu as pltpu
from jax.sharding import PartitionSpec as P

MESH = pl.DeviceIdType.MESH
LAST = (((1,), (1,)), ((), ()))
FIRST = (((0,), (0,)), ((), ()))
F32 = jnp.float32
BF16 = jnp.bfloat16
TILE = 256
GRANT = 57 * 1024 * 1024


def flip(index, k):
    if k == 0:
        return index
    if k == 1:
        return index + 1 - 2 * lax.rem(index, 2)
    if k == 2:
        return lax.rem(index + 2, 4)
    return 3 - index


def remote(src, dst, send_sem, recv_sem, device):
    return pltpu.make_async_remote_copy(
        src_ref=src, dst_ref=dst, send_sem=send_sem, recv_sem=recv_sem, device_id=device, device_id_type=MESH
    )


def finish(*refs):
    sources, results, held = refs[:4], refs[4:8], refs[8:12]
    in_sem, out_sem = refs[12:]
    loads, stores = [], []
    for src, dst, kept in zip(sources, results, held):
        half = src.shape[0] // 2
        for part in range(2):
            rows = pl.ds(part * half, half)
            index = len(loads)
            loads.append(pltpu.make_async_copy(src.at[rows], kept.at[rows], in_sem.at[index]))
            stores.append(pltpu.make_async_copy(kept.at[rows], dst.at[rows], out_sem.at[index]))
    for load in loads:
        load.start()
    for load, store in zip(loads, stores):
        load.wait()
        store.start()
    for store in stores:
        store.wait()


def kernel(
    labels,
    tokens_hbm,
    upstream_hbm,
    up_hbm,
    down_hbm,
    layer_out,
    grad_tokens_out,
    grad_up_out,
    grad_down_out,
    rows_in,
    up,
    down,
    routed,
    gathered,
    hidden,
    slope_kept,
    pre_grad,
    parts,
    parts_in,
    summed,
    returned,
    grad_up,
    grad_down,
    grad_down_turned,
    shares,
    load_sem,
    store_sem,
    z_send,
    z_recv,
    x_send,
    x_recv,
    y_send,
    y_recv,
    s_send,
    s_recv,
    p_send,
    p_recv,
    r_send,
    r_recv,
    h_send,
    h_recv,
):
    dp = lax.axis_index("dp")
    me = lax.axis_index("expert")
    core = lax.axis_index("mp")
    other = 1 - core
    tok_rows, width = rows_in.shape[1], rows_in.shape[2]
    blocks_dev = labels.shape[1]
    block = tok_rows // blocks_dev
    slots = routed.shape[1]
    half = slots // 2
    piece = half // 4
    share = grad_up.shape[0]
    units = up.shape[1]

    loads = [
        pltpu.make_async_copy(tokens_hbm, rows_in.at[0], load_sem.at[0]),
        pltpu.make_async_copy(upstream_hbm, rows_in.at[1], load_sem.at[1]),
        pltpu.make_async_copy(up_hbm, up, load_sem.at[2]),
        pltpu.make_async_copy(down_hbm, down, load_sem.at[3]),
    ]
    for load in loads:
        load.start()

    x_peer = {"dp": flip(dp, 1)}
    y_peer = {"dp": flip(dp, 2)}
    sibling = {"mp": other}
    z_peers = [{"expert": flip(me, k)} for k in range(4)]
    barrier = pltpu.get_barrier_semaphore()
    for peer in z_peers[1:] + [x_peer, y_peer, sibling]:
        pl.semaphore_signal(barrier, inc=1, device_id=peer, device_id_type=MESH)

    experts_at = lax.broadcasted_iota(jnp.int32, (128, blocks_dev), 0)
    named = (labels[...] == experts_at).astype(F32)
    row_at = lax.broadcasted_iota(jnp.int32, (tok_rows, blocks_dev), 0)
    first_row = lax.broadcasted_iota(jnp.int32, (tok_rows, blocks_dev), 1) * block
    in_block = jnp.logical_and(row_at >= first_row, row_at < first_row + block)
    before = row_at >= first_row + block
    row_expert = lax.dot_general(in_block.astype(F32), named, LAST, preferred_element_type=F32)
    row_rank = lax.dot_general(before.astype(F32), named, LAST, preferred_element_type=F32)
    start = lax.broadcasted_iota(jnp.int32, (tok_rows, 128), 1).astype(F32) * piece
    first_slot = jnp.sum(row_expert * start, axis=1, keepdims=True)
    place = jnp.sum(row_expert * (block * row_rank), axis=1, keepdims=True)
    place += jnp.sum(jnp.where(in_block, row_at - first_row, 0).astype(F32), axis=1, keepdims=True)
    slot_of_row = first_slot + place + jnp.where(place >= piece, float(half - piece), 0.0)
    slot_at = lax.broadcasted_iota(jnp.int32, (tok_rows, slots), 1).astype(F32)
    picks = (slot_of_row == slot_at).astype(BF16)

    def one(side, k):
        return pl.ds(pl.multiple_of(side * half + flip(me, k) * piece, piece), piece)

    def pair(side, p):
        q = lax.div(me, 2)
        at = q if p == 0 else 1 - q
        return pl.ds(pl.multiple_of(side * half + at * (2 * piece), 2 * piece), 2 * piece)

    sent = []

    def go(src, dst, send_sem, recv_sem, peer):
        copy = remote(src, dst, send_sem, recv_sem, peer)
        copy.start()
        sent.append(copy)

    def arrived(dst, send_sem, recv_sem, peer):
        remote(dst, dst, send_sem, recv_sem, peer).wait_recv()

    def route(a):
        loads[a].wait()
        rows_lo = rows_in[a].astype(BF16)
        routed[a] = lax.dot_general(picks, rows_lo, FIRST, preferred_element_type=F32).astype(BF16)

    def dispatch(a):
        for k in (1, 2, 3):
            go(
                routed.at[a, one(core, k)],
                gathered.at[a, dp, one(core, 0)],
                z_send.at[a, k],
                z_recv.at[a, k],
                z_peers[k],
            )
        gathered[a, dp, one(core, 0), :] = routed[a, one(core, 0), :]

    def block_at(a, rel, p, side=None):
        return gathered.at[a, flip(dp, rel), pair(core if side is None else side, p)]

    def to_sibling(a, rel, p):
        go(block_at(a, rel, p), block_at(a, rel, p), s_send.at[a, rel, p], s_recv.at[a, rel, p], sibling)

    def from_sibling(a, rel):
        for p in range(2):
            arrived(block_at(a, rel, p, other), s_send.at[a, rel, p], s_recv.at[a, rel, p], sibling)

    def spread(a, p):
        for k in (2 * p, 2 * p + 1):
            if k:
                arrived(gathered.at[a, dp, one(core, k)], z_send.at[a, k], z_recv.at[a, k], z_peers[k])
        to_sibling(a, 0, p)
        go(block_at(a, 0, p), block_at(a, 0, p), x_send.at[a, p], x_recv.at[a, p], x_peer)
        go(block_at(a, 0, p), block_at(a, 0, p), y_send.at[a, p], y_recv.at[a, p], y_peer)

    def pass_on(a, p):
        arrived(block_at(a, 1, p), x_send.at[a, p], x_recv.at[a, p], x_peer)
        if p == 0:
            go(block_at(a, 1, 0), block_at(a, 1, 0), y_send.at[a, 2], y_recv.at[a, 2], y_peer)
        to_sibling(a, 1, p)
        arrived(block_at(a, 2, p), y_send.at[a, p], y_recv.at[a, p], y_peer)
        if p == 1:
            go(block_at(a, 2, 1), block_at(a, 2, 1), x_send.at[a, 2], x_recv.at[a, 2], x_peer)
        to_sibling(a, 2, p)

    def from_corner(a):
        arrived(block_at(a, 3, 0), y_send.at[a, 2], y_recv.at[a, 2], y_peer)
        to_sibling(a, 3, 0)
        arrived(block_at(a, 3, 1), x_send.at[a, 2], x_recv.at[a, 2], x_peer)
        to_sibling(a, 3, 1)

    mine_cols = pl.ds(pl.multiple_of(dp * share, share), share)

    def activation(value):
        scale = 0.7978845608028654
        square = value * value
        turn = jnp.tanh(value * (scale + (scale * 0.044715) * square))
        cdf = 0.5 + 0.5 * turn
        slope = cdf + value * (0.5 - 0.5 * turn * turn) * (scale + (3 * scale * 0.044715) * square)
        return (value * cdf).astype(BF16), slope

    def tiles(total, step):
        for index in range(total // TILE):
            step(pl.ds(index * TILE, TILE))

    def forward(cols):
        value = jnp.dot(gathered[0, dp], up[:, cols], preferred_element_type=F32)
        hidden[:, cols], slope_kept[:, cols] = activation(value)

    def mix(cols):
        parts[0, :, cols] = jnp.dot(hidden[...], down[:, cols], preferred_element_type=F32).astype(BF16)

    def backward(cols):
        back = lax.dot_general(gathered[1, dp], down[cols, :], LAST, preferred_element_type=F32)
        pre_grad[:, cols] = (back * slope_kept[:, cols]).astype(BF16)

    def unmix(cols):
        parts[1, :, cols] = lax.dot_general(
            pre_grad[...], up[cols, :], LAST, preferred_element_type=F32
        ).astype(BF16)

    def turn_shares(rel):
        for a in range(2):
            shares[a] = gathered[a, flip(dp, rel), :, mine_cols].T

    def own_grads(cols):
        grad_up[:, cols] = jnp.dot(shares[0], pre_grad[:, cols], preferred_element_type=F32)
        grad_down_turned[:, cols] = jnp.dot(shares[1], hidden[:, cols], preferred_element_type=F32)

    def other_grads(rel):
        at = flip(dp, rel)
        turn_shares(rel)

        def step(cols):
            value = jnp.dot(gathered[0, at], up[:, cols], preferred_element_type=F32)
            back = lax.dot_general(gathered[1, at], down[cols, :], LAST, preferred_element_type=F32)
            hidden_lo, slope = activation(value)
            grad_lo = (back * slope).astype(BF16)
            grad_up[:, cols] += jnp.dot(shares[0], grad_lo, preferred_element_type=F32)
            grad_down_turned[:, cols] += jnp.dot(shares[1], hidden_lo, preferred_element_type=F32)

        tiles(units, step)

    def turn_down(cols):
        grad_down[cols, :] = grad_down_turned[:, cols].T

    def swap(a):
        theirs = pl.ds(pl.multiple_of(other * half, half), half)
        go(parts.at[a, theirs], parts_in.at[a], p_send.at[a], p_recv.at[a], sibling)

    def send_home(a):
        arrived(parts_in.at[a], p_send.at[a], p_recv.at[a], sibling)
        ours = pl.ds(pl.multiple_of(core * half, half), half)
        summed[a] = (parts[a, ours, :].astype(F32) + parts_in[a].astype(F32)).astype(BF16)
        for k in (2, 3, 1):
            go(
                summed.at[a, pl.ds(pl.multiple_of(flip(me, k) * piece, piece), piece)],
                returned.at[a, one(core, 0)],
                r_send.at[a, k],
                r_recv.at[a, k],
                z_peers[k],
            )
        returned[a, one(core, 0), :] = summed[a, pl.ds(pl.multiple_of(me * piece, piece), piece), :]

    def reach_home(a, p):
        for k in (2 * p, 2 * p + 1):
            if k:
                arrived(returned.at[a, one(core, k)], r_send.at[a, k], r_recv.at[a, k], z_peers[k])
        block = returned.at[a, pair(core, p)]
        go(block, block, h_send.at[a, p], h_recv.at[a, p], sibling)

    stores = []

    def store(src, dst):
        copy = pltpu.make_async_copy(src, dst, store_sem.at[len(stores)])
        copy.start()
        stores.append(copy)

    def add_home(a, out):
        for p in range(2):
            arrived(returned.at[a, pair(other, p)], h_send.at[a, p], h_recv.at[a, p], sibling)
        rows_in[a] += jnp.dot(picks, returned[a], preferred_element_type=F32)
        store(rows_in.at[a], out)

    route(0)
    pl.semaphore_wait(barrier, 6)
    dispatch(0)
    route(1)
    spread(0, 0)
    dispatch(1)
    pass_on(0, 0)
    spread(0, 1)
    spread(1, 0)
    loads[2].wait()
    loads[3].wait()
    from_sibling(0, 0)
    tiles(units, forward)
    tiles(width, mix)
    swap(0)
    pass_on(0, 1)
    send_home(0)
    pass_on(1, 0)
    spread(1, 1)
    from_sibling(1, 0)
    tiles(units, backward)
    tiles(width, unmix)
    swap(1)
    pass_on(1, 1)
    turn_shares(0)
    tiles(units, own_grads)
    send_home(1)
    for a in range(2):
        from_sibling(a, 1)
    other_grads(1)
    from_corner(0)
    from_corner(1)
    for a in range(2):
        from_sibling(a, 2)
    other_grads(2)
    reach_home(0, 0)
    reach_home(0, 1)
    for a in range(2):
        from_sibling(a, 3)
    other_grads(3)
    store(grad_up, grad_up_out)
    tiles(units, turn_down)
    store(grad_down, grad_down_out)
    reach_home(1, 0)
    add_home(0, layer_out)
    reach_home(1, 1)
    add_home(1, grad_tokens_out)
    for copy in sent:
        copy.wait_send()
    for copy in stores:
        copy.wait()


def fused_body(tokens, block_experts, weight_up, weight_down, upstream):
    tok_rows, width = tokens.shape
    blocks_dev = block_experts.shape[0]
    units = weight_up.shape[2]
    slots = 2 * tok_rows
    half = slots // 2
    share = width // 4
    in_hbm = pl.BlockSpec(memory_space=pltpu.HBM)
    anywhere = pl.BlockSpec(memory_space=pl.ANY)
    flops = 2 * slots * width * units * 12
    results = (
        jax.ShapeDtypeStruct((tok_rows, width), F32),
        jax.ShapeDtypeStruct((tok_rows, width), F32),
        jax.ShapeDtypeStruct((share, units), F32),
        jax.ShapeDtypeStruct((units, share), F32),
    )
    held = pl.pallas_call(
        kernel,
        out_shape=results,
        in_specs=[pl.BlockSpec(memory_space=pltpu.VMEM)] + [in_hbm] * 4,
        out_specs=(anywhere,) * 4,
        scratch_shapes=[
            pltpu.VMEM((2, tok_rows, width), F32),
            pltpu.VMEM((width, units), BF16),
            pltpu.VMEM((units, width), BF16),
            pltpu.VMEM((2, slots, width), BF16),
            pltpu.VMEM((2, 4, slots, width), BF16),
            pltpu.VMEM((slots, units), BF16),
            pltpu.VMEM((slots, units), F32),
            pltpu.VMEM((slots, units), BF16),
            pltpu.VMEM((2, slots, width), BF16),
            pltpu.VMEM((2, half, width), BF16),
            pltpu.VMEM((2, half, width), BF16),
            pltpu.VMEM((2, slots, width), BF16),
            pltpu.VMEM((share, units), F32),
            pltpu.VMEM((units, share), F32),
            pltpu.VMEM((share, units), F32),
            pltpu.VMEM((2, share, slots), BF16),
            pltpu.SemaphoreType.DMA((4,)),
            pltpu.SemaphoreType.DMA((4,)),
            pltpu.SemaphoreType.DMA((2, 4)),
            pltpu.SemaphoreType.DMA((2, 4)),
            pltpu.SemaphoreType.DMA((2, 3)),
            pltpu.SemaphoreType.DMA((2, 3)),
            pltpu.SemaphoreType.DMA((2, 3)),
            pltpu.SemaphoreType.DMA((2, 3)),
            pltpu.SemaphoreType.DMA((2, 4, 2)),
            pltpu.SemaphoreType.DMA((2, 4, 2)),
            pltpu.SemaphoreType.DMA((2,)),
            pltpu.SemaphoreType.DMA((2,)),
            pltpu.SemaphoreType.DMA((2, 4)),
            pltpu.SemaphoreType.DMA((2, 4)),
            pltpu.SemaphoreType.DMA((2, 2)),
            pltpu.SemaphoreType.DMA((2, 2)),
        ],
        compiler_params=pltpu.CompilerParams(
            collective_id=0, has_side_effects=True, vmem_limit_bytes=GRANT
        ),
        cost_estimate=pl.CostEstimate(flops=flops, bytes_accessed=8 << 20, transcendentals=slots * units * 4),
    )(block_experts.reshape(1, blocks_dev), tokens, upstream, weight_up[0], weight_down[0])
    layer_output, grad_tokens, grad_up, grad_down = pl.pallas_call(
        finish,
        out_shape=results,
        in_specs=[anywhere] * 4,
        out_specs=(in_hbm,) * 4,
        scratch_shapes=[pltpu.VMEM(result.shape, F32) for result in results]
        + [pltpu.SemaphoreType.DMA((8,)), pltpu.SemaphoreType.DMA((8,))],
        compiler_params=pltpu.CompilerParams(vmem_limit_bytes=GRANT),
        cost_estimate=pl.CostEstimate(flops=0, bytes_accessed=3 << 20, transcendentals=0),
    )(*held)
    return layer_output, grad_tokens, grad_up[None], grad_down[None]


def plain_body(tokens, block_experts, weight_up, weight_down, upstream):
    experts = lax.axis_size("expert")
    blocks_dev = block_experts.shape[0]
    tok_rows = tokens.shape[0]
    width = tokens.shape[1]
    block = tok_rows // blocks_dev
    capacity = max(1, blocks_dev * 2 // experts)
    slot_total = experts * capacity
    labels = block_experts[:, 0]
    order = jnp.arange(blocks_dev, dtype=jnp.int32)
    earlier = order[None, :] < order[:, None]
    matches = labels[:, None] == labels[None, :]
    block_rank = jnp.sum(jnp.logical_and(matches, earlier).astype(jnp.int32), axis=1)
    slot_of_block = labels * capacity + block_rank
    slot_match = slot_of_block[None, :] == jnp.arange(slot_total, dtype=jnp.int32)[:, None]
    source_block = jnp.sum(jnp.where(slot_match, order[None, :], 0), axis=1)
    occupied = jnp.any(slot_match, axis=1)

    def dispatch(rows_lo):
        blocks = rows_lo.reshape(blocks_dev, block, width)
        picked = jnp.take(blocks, source_block, axis=0)
        filled = jnp.where(occupied[:, None, None], picked, jnp.zeros((), rows_lo.dtype))
        outgoing = filled.reshape(experts, capacity * block, width)
        arrived = lax.all_to_all(outgoing, "expert", split_axis=0, concat_axis=0, tiled=True)
        return arrived.reshape(-1, width)

    def bring_home(partial_value):
        shaped = partial_value.reshape(experts, capacity * block, width)
        returned = lax.all_to_all(
            shaped.astype(jnp.bfloat16), "expert", split_axis=0, concat_axis=0, tiled=True
        ).astype(shaped.dtype)
        mine = jnp.take(returned.reshape(slot_total, block, width), slot_of_block, axis=0)
        result = lax.psum(mine.reshape(tok_rows, width).astype(jnp.bfloat16), "mp").astype(
            jnp.float32
        )
        return result

    up_matrix = weight_up[0]
    down_matrix = weight_down[0]
    contract_last = (((1,), (1,)), ((), ()))
    contract_first = (((0,), (0,)), ((), ()))
    routed_lo = dispatch(tokens.astype(jnp.bfloat16))
    pre_act = jnp.dot(routed_lo, up_matrix, preferred_element_type=jnp.float32)
    hidden = jax.nn.gelu(pre_act).astype(jnp.bfloat16)
    mixed_part = jnp.dot(hidden, down_matrix, preferred_element_type=jnp.float32)
    layer_output = tokens + bring_home(mixed_part)
    routed_up = dispatch(upstream.astype(jnp.bfloat16))
    hidden_grad = lax.dot_general(
        routed_up, down_matrix, contract_last, preferred_element_type=jnp.float32
    )
    unused, gelu_back = jax.vjp(jax.nn.gelu, pre_act)
    pre_grad = gelu_back(hidden_grad)[0].astype(jnp.bfloat16)
    token_part = lax.dot_general(
        pre_grad, up_matrix, contract_last, preferred_element_type=jnp.float32
    )
    up_part = lax.dot_general(
        routed_lo, pre_grad, contract_first, preferred_element_type=jnp.float32
    )
    down_part = lax.dot_general(
        hidden, routed_up, contract_first, preferred_element_type=jnp.float32
    )
    grad_tokens = upstream + bring_home(token_part)
    grad_up, grad_down = (
        lax.psum_scatter(
            up_part[None].astype(jnp.bfloat16), "dp", scatter_dimension=1, tiled=True
        ).astype(jnp.float32),
        lax.psum_scatter(
            down_part[None].astype(jnp.bfloat16), "dp", scatter_dimension=2, tiled=True
        ).astype(jnp.float32),
    )
    return (layer_output, grad_tokens, grad_up, grad_down)


def solution(mesh):
    placed = (
        P(("dp", "expert"), None),
        P(("dp", "expert"), None),
        P("expert", None, "mp"),
        P("expert", "mp", None),
        P(("dp", "expert"), None),
    )

    def body(tokens, block_experts, weight_up, weight_down, upstream):
        tok_rows, width = tokens.shape
        blocks_dev = block_experts.shape[0]
        fits = (
            (mesh.shape["dp"], mesh.shape["expert"], mesh.shape["mp"]) == (4, 4, 2)
            and blocks_dev % 2 == 0
            and (tok_rows // 4) % 16 == 0
            and width % (4 * TILE) == 0
            and weight_up.shape[2] % TILE == 0
        )
        chosen = fused_body if fits else plain_body
        return chosen(tokens, block_experts, weight_up, weight_down, upstream)

    return jax.shard_map(
        body,
        mesh=mesh,
        in_specs=placed,
        out_specs=(
            P(("dp", "expert"), None),
            P(("dp", "expert"), None),
            P("expert", "dp", "mp"),
            P("expert", "mp", "dp"),
        ),
        check_vma=False,
    )
```

```python
import jax
import jax.numpy as jnp
from jax import lax
from jax.experimental import pallas as pl
from jax.experimental.pallas import tpu as pltpu
from jax.sharding import PartitionSpec as P

MESH = pl.DeviceIdType.MESH
LAST = (((1,), (1,)), ((), ()))
FIRST = (((0,), (0,)), ((), ()))
F32 = jnp.float32
BF16 = jnp.bfloat16
TILE = 256
GRANT = 57 * 1024 * 1024


def flip(index, k):
    if k == 0:
        return index
    if k == 1:
        return index + 1 - 2 * lax.rem(index, 2)
    if k == 2:
        return lax.rem(index + 2, 4)
    return 3 - index


def remote(src, dst, send_sem, recv_sem, device):
    return pltpu.make_async_remote_copy(
        src_ref=src, dst_ref=dst, send_sem=send_sem, recv_sem=recv_sem, device_id=device, device_id_type=MESH
    )


def finish(*refs):
    sources, results, held = refs[:4], refs[4:8], refs[8:12]
    in_sem, out_sem = refs[12:]
    loads, stores = [], []
    for src, dst, kept in zip(sources, results, held):
        half = src.shape[0] // 2
        for part in range(2):
            rows = pl.ds(part * half, half)
            index = len(loads)
            loads.append(pltpu.make_async_copy(src.at[rows], kept.at[rows], in_sem.at[index]))
            stores.append(pltpu.make_async_copy(kept.at[rows], dst.at[rows], out_sem.at[index]))
    for load in loads:
        load.start()
    for load, store in zip(loads, stores):
        load.wait()
        store.start()
    for store in stores:
        store.wait()


def kernel(
    labels,
    tokens_hbm,
    upstream_hbm,
    up_hbm,
    down_hbm,
    layer_out,
    grad_tokens_out,
    grad_up_out,
    grad_down_out,
    rows_in,
    up,
    down,
    routed,
    gathered,
    hidden,
    slope_kept,
    pre_grad,
    parts,
    parts_in,
    summed,
    returned,
    grad_up,
    grad_down,
    grad_down_turned,
    shares,
    load_sem,
    store_sem,
    z_send,
    z_recv,
    x_send,
    x_recv,
    y_send,
    y_recv,
    s_send,
    s_recv,
    p_send,
    p_recv,
    r_send,
    r_recv,
    h_send,
    h_recv,
):
    dp = lax.axis_index("dp")
    me = lax.axis_index("expert")
    core = lax.axis_index("mp")
    other = 1 - core
    tok_rows, width = rows_in.shape[1], rows_in.shape[2]
    blocks_dev = labels.shape[1]
    block = tok_rows // blocks_dev
    slots = routed.shape[1]
    half = slots // 2
    piece = half // 4
    share = grad_up.shape[0]
    units = up.shape[1]

    loads = [
        pltpu.make_async_copy(tokens_hbm, rows_in.at[0], load_sem.at[0]),
        pltpu.make_async_copy(upstream_hbm, rows_in.at[1], load_sem.at[1]),
        pltpu.make_async_copy(up_hbm, up, load_sem.at[2]),
        pltpu.make_async_copy(down_hbm, down, load_sem.at[3]),
    ]
    for load in loads:
        load.start()

    x_peer = {"dp": flip(dp, 1)}
    y_peer = {"dp": flip(dp, 2)}
    sibling = {"mp": other}
    z_peers = [{"expert": flip(me, k)} for k in range(4)]
    barrier = pltpu.get_barrier_semaphore()
    for peer in z_peers[1:] + [x_peer, y_peer, sibling]:
        pl.semaphore_signal(barrier, inc=1, device_id=peer, device_id_type=MESH)

    experts_at = lax.broadcasted_iota(jnp.int32, (128, blocks_dev), 0)
    named = (labels[...] == experts_at).astype(F32)
    row_at = lax.broadcasted_iota(jnp.int32, (tok_rows, blocks_dev), 0)
    first_row = lax.broadcasted_iota(jnp.int32, (tok_rows, blocks_dev), 1) * block
    in_block = jnp.logical_and(row_at >= first_row, row_at < first_row + block)
    before = row_at >= first_row + block
    row_expert = lax.dot_general(in_block.astype(F32), named, LAST, preferred_element_type=F32)
    row_rank = lax.dot_general(before.astype(F32), named, LAST, preferred_element_type=F32)
    start = lax.broadcasted_iota(jnp.int32, (tok_rows, 128), 1).astype(F32) * piece
    first_slot = jnp.sum(row_expert * start, axis=1, keepdims=True)
    place = jnp.sum(row_expert * (block * row_rank), axis=1, keepdims=True)
    place += jnp.sum(jnp.where(in_block, row_at - first_row, 0).astype(F32), axis=1, keepdims=True)
    slot_of_row = first_slot + place + jnp.where(place >= piece, float(half - piece), 0.0)
    slot_at = lax.broadcasted_iota(jnp.int32, (tok_rows, slots), 1).astype(F32)
    picks = (slot_of_row == slot_at).astype(BF16)

    def one(side, k):
        return pl.ds(pl.multiple_of(side * half + flip(me, k) * piece, piece), piece)

    def pair(side, p):
        q = lax.div(me, 2)
        at = q if p == 0 else 1 - q
        return pl.ds(pl.multiple_of(side * half + at * (2 * piece), 2 * piece), 2 * piece)

    sent = []

    def go(src, dst, send_sem, recv_sem, peer):
        copy = remote(src, dst, send_sem, recv_sem, peer)
        copy.start()
        sent.append(copy)

    def arrived(dst, send_sem, recv_sem, peer):
        remote(dst, dst, send_sem, recv_sem, peer).wait_recv()

    def route(a):
        loads[a].wait()
        rows_lo = rows_in[a].astype(BF16)
        routed[a] = lax.dot_general(picks, rows_lo, FIRST, preferred_element_type=F32).astype(BF16)

    def dispatch(a, k):
        go(
            routed.at[a, one(core, k)],
            gathered.at[a, dp, one(core, 0)],
            z_send.at[a, k],
            z_recv.at[a, k],
            z_peers[k],
        )

    def keep_own(a):
        gathered[a, dp, one(core, 0), :] = routed[a, one(core, 0), :]

    def block_at(a, rel, p, side=None):
        return gathered.at[a, flip(dp, rel), pair(core if side is None else side, p)]

    def to_sibling(a, rel, p):
        go(block_at(a, rel, p), block_at(a, rel, p), s_send.at[a, rel, p], s_recv.at[a, rel, p], sibling)

    def from_sibling(a, rel):
        for p in range(2):
            arrived(block_at(a, rel, p, other), s_send.at[a, rel, p], s_recv.at[a, rel, p], sibling)

    def spread(a, p):
        for k in (2 * p, 2 * p + 1):
            if k:
                arrived(gathered.at[a, dp, one(core, k)], z_send.at[a, k], z_recv.at[a, k], z_peers[k])
                if a == 0:
                    dispatch(1, k)
        to_sibling(a, 0, p)
        go(block_at(a, 0, p), block_at(a, 0, p), x_send.at[a, p], x_recv.at[a, p], x_peer)
        go(block_at(a, 0, p), block_at(a, 0, p), y_send.at[a, p], y_recv.at[a, p], y_peer)

    def pass_on(a, p):
        arrived(block_at(a, 1, p), x_send.at[a, p], x_recv.at[a, p], x_peer)
        if p == 0:
            go(block_at(a, 1, 0), block_at(a, 1, 0), y_send.at[a, 2], y_recv.at[a, 2], y_peer)
        to_sibling(a, 1, p)
        arrived(block_at(a, 2, p), y_send.at[a, p], y_recv.at[a, p], y_peer)
        if p == 1:
            go(block_at(a, 2, 1), block_at(a, 2, 1), x_send.at[a, 2], x_recv.at[a, 2], x_peer)
        to_sibling(a, 2, p)

    def from_corner(a):
        arrived(block_at(a, 3, 0), y_send.at[a, 2], y_recv.at[a, 2], y_peer)
        to_sibling(a, 3, 0)
        arrived(block_at(a, 3, 1), x_send.at[a, 2], x_recv.at[a, 2], x_peer)
        to_sibling(a, 3, 1)

    mine_cols = pl.ds(pl.multiple_of(dp * share, share), share)

    def activation(value):
        scale = 0.7978845608028654
        square = value * value
        turn = jnp.tanh(value * (scale + (scale * 0.044715) * square))
        cdf = 0.5 + 0.5 * turn
        slope = cdf + value * (0.5 - 0.5 * turn * turn) * (scale + (3 * scale * 0.044715) * square)
        return (value * cdf).astype(BF16), slope

    def tiles(total, step):
        for index in range(total // TILE):
            step(pl.ds(index * TILE, TILE))

    def forward(cols):
        value = jnp.dot(gathered[0, dp], up[:, cols], preferred_element_type=F32)
        hidden[:, cols], slope_kept[:, cols] = activation(value)

    def mix(cols):
        parts[0, :, cols] = jnp.dot(hidden[...], down[:, cols], preferred_element_type=F32).astype(BF16)

    def backward(cols):
        back = lax.dot_general(gathered[1, dp], down[cols, :], LAST, preferred_element_type=F32)
        pre_grad[:, cols] = (back * slope_kept[:, cols]).astype(BF16)

    def unmix(cols):
        parts[1, :, cols] = lax.dot_general(
            pre_grad[...], up[cols, :], LAST, preferred_element_type=F32
        ).astype(BF16)

    def turn_shares(rel):
        for a in range(2):
            shares[a] = gathered[a, flip(dp, rel), :, mine_cols].T

    def own_grads(cols):
        grad_up[:, cols] = jnp.dot(shares[0], pre_grad[:, cols], preferred_element_type=F32)
        grad_down_turned[:, cols] = jnp.dot(shares[1], hidden[:, cols], preferred_element_type=F32)

    def other_grads(rel):
        at = flip(dp, rel)
        turn_shares(rel)

        def step(cols):
            value = jnp.dot(gathered[0, at], up[:, cols], preferred_element_type=F32)
            back = lax.dot_general(gathered[1, at], down[cols, :], LAST, preferred_element_type=F32)
            hidden_lo, slope = activation(value)
            grad_lo = (back * slope).astype(BF16)
            grad_up[:, cols] += jnp.dot(shares[0], grad_lo, preferred_element_type=F32)
            grad_down_turned[:, cols] += jnp.dot(shares[1], hidden_lo, preferred_element_type=F32)

        tiles(units, step)

    def turn_down(cols):
        grad_down[cols, :] = grad_down_turned[:, cols].T

    def swap(a):
        theirs = pl.ds(pl.multiple_of(other * half, half), half)
        go(parts.at[a, theirs], parts_in.at[a], p_send.at[a], p_recv.at[a], sibling)

    def send_home(a):
        arrived(parts_in.at[a], p_send.at[a], p_recv.at[a], sibling)
        ours = pl.ds(pl.multiple_of(core * half, half), half)
        summed[a] = (parts[a, ours, :].astype(F32) + parts_in[a].astype(F32)).astype(BF16)
        for k in (2, 3, 1):
            go(
                summed.at[a, pl.ds(pl.multiple_of(flip(me, k) * piece, piece), piece)],
                returned.at[a, one(core, 0)],
                r_send.at[a, k],
                r_recv.at[a, k],
                z_peers[k],
            )
        returned[a, one(core, 0), :] = summed[a, pl.ds(pl.multiple_of(me * piece, piece), piece), :]

    def reach_home(a, p):
        for k in (2 * p, 2 * p + 1):
            if k:
                arrived(returned.at[a, one(core, k)], r_send.at[a, k], r_recv.at[a, k], z_peers[k])
        block = returned.at[a, pair(core, p)]
        go(block, block, h_send.at[a, p], h_recv.at[a, p], sibling)

    stores = []

    def store(src, dst):
        copy = pltpu.make_async_copy(src, dst, store_sem.at[len(stores)])
        copy.start()
        stores.append(copy)

    def add_home(a, out):
        for p in range(2):
            arrived(returned.at[a, pair(other, p)], h_send.at[a, p], h_recv.at[a, p], sibling)
        rows_in[a] += jnp.dot(picks, returned[a], preferred_element_type=F32)
        store(rows_in.at[a], out)

    route(0)
    pl.semaphore_wait(barrier, 6)
    for k in (1, 2, 3):
        dispatch(0, k)
    keep_own(0)
    route(1)
    keep_own(1)
    spread(0, 0)
    pass_on(0, 0)
    spread(0, 1)
    spread(1, 0)
    loads[2].wait()
    loads[3].wait()
    from_sibling(0, 0)
    tiles(units, forward)
    tiles(width, mix)
    swap(0)
    pass_on(0, 1)
    send_home(0)
    pass_on(1, 0)
    spread(1, 1)
    from_sibling(1, 0)
    tiles(units, backward)
    tiles(width, unmix)
    swap(1)
    pass_on(1, 1)
    turn_shares(0)
    tiles(units, own_grads)
    send_home(1)
    for a in range(2):
        from_sibling(a, 1)
    other_grads(1)
    from_corner(0)
    from_corner(1)
    for a in range(2):
        from_sibling(a, 2)
    other_grads(2)
    reach_home(0, 0)
    reach_home(0, 1)
    for a in range(2):
        from_sibling(a, 3)
    other_grads(3)
    store(grad_up, grad_up_out)
    tiles(units, turn_down)
    store(grad_down, grad_down_out)
    reach_home(1, 0)
    add_home(0, layer_out)
    reach_home(1, 1)
    add_home(1, grad_tokens_out)
    for copy in sent:
        copy.wait_send()
    for copy in stores:
        copy.wait()


def fused_body(tokens, block_experts, weight_up, weight_down, upstream):
    tok_rows, width = tokens.shape
    blocks_dev = block_experts.shape[0]
    units = weight_up.shape[2]
    slots = 2 * tok_rows
    half = slots // 2
    share = width // 4
    in_hbm = pl.BlockSpec(memory_space=pltpu.HBM)
    anywhere = pl.BlockSpec(memory_space=pl.ANY)
    flops = 2 * slots * width * units * 12
    results = (
        jax.ShapeDtypeStruct((tok_rows, width), F32),
        jax.ShapeDtypeStruct((tok_rows, width), F32),
        jax.ShapeDtypeStruct((share, units), F32),
        jax.ShapeDtypeStruct((units, share), F32),
    )
    held = pl.pallas_call(
        kernel,
        out_shape=results,
        in_specs=[pl.BlockSpec(memory_space=pltpu.VMEM)] + [in_hbm] * 4,
        out_specs=(anywhere,) * 4,
        scratch_shapes=[
            pltpu.VMEM((2, tok_rows, width), F32),
            pltpu.VMEM((width, units), BF16),
            pltpu.VMEM((units, width), BF16),
            pltpu.VMEM((2, slots, width), BF16),
            pltpu.VMEM((2, 4, slots, width), BF16),
            pltpu.VMEM((slots, units), BF16),
            pltpu.VMEM((slots, units), F32),
            pltpu.VMEM((slots, units), BF16),
            pltpu.VMEM((2, slots, width), BF16),
            pltpu.VMEM((2, half, width), BF16),
            pltpu.VMEM((2, half, width), BF16),
            pltpu.VMEM((2, slots, width), BF16),
            pltpu.VMEM((share, units), F32),
            pltpu.VMEM((units, share), F32),
            pltpu.VMEM((share, units), F32),
            pltpu.VMEM((2, share, slots), BF16),
            pltpu.SemaphoreType.DMA((4,)),
            pltpu.SemaphoreType.DMA((4,)),
            pltpu.SemaphoreType.DMA((2, 4)),
            pltpu.SemaphoreType.DMA((2, 4)),
            pltpu.SemaphoreType.DMA((2, 3)),
            pltpu.SemaphoreType.DMA((2, 3)),
            pltpu.SemaphoreType.DMA((2, 3)),
            pltpu.SemaphoreType.DMA((2, 3)),
            pltpu.SemaphoreType.DMA((2, 4, 2)),
            pltpu.SemaphoreType.DMA((2, 4, 2)),
            pltpu.SemaphoreType.DMA((2,)),
            pltpu.SemaphoreType.DMA((2,)),
            pltpu.SemaphoreType.DMA((2, 4)),
            pltpu.SemaphoreType.DMA((2, 4)),
            pltpu.SemaphoreType.DMA((2, 2)),
            pltpu.SemaphoreType.DMA((2, 2)),
        ],
        compiler_params=pltpu.CompilerParams(
            collective_id=0, has_side_effects=True, vmem_limit_bytes=GRANT
        ),
        cost_estimate=pl.CostEstimate(flops=flops, bytes_accessed=8 << 20, transcendentals=slots * units * 4),
    )(block_experts.reshape(1, blocks_dev), tokens, upstream, weight_up[0], weight_down[0])
    layer_output, grad_tokens, grad_up, grad_down = pl.pallas_call(
        finish,
        out_shape=results,
        in_specs=[anywhere] * 4,
        out_specs=(in_hbm,) * 4,
        scratch_shapes=[pltpu.VMEM(result.shape, F32) for result in results]
        + [pltpu.SemaphoreType.DMA((8,)), pltpu.SemaphoreType.DMA((8,))],
        compiler_params=pltpu.CompilerParams(vmem_limit_bytes=GRANT),
        cost_estimate=pl.CostEstimate(flops=0, bytes_accessed=3 << 20, transcendentals=0),
    )(*held)
    return layer_output, grad_tokens, grad_up[None], grad_down[None]


def plain_body(tokens, block_experts, weight_up, weight_down, upstream):
    experts = lax.axis_size("expert")
    blocks_dev = block_experts.shape[0]
    tok_rows = tokens.shape[0]
    width = tokens.shape[1]
    block = tok_rows // blocks_dev
    capacity = max(1, blocks_dev * 2 // experts)
    slot_total = experts * capacity
    labels = block_experts[:, 0]
    order = jnp.arange(blocks_dev, dtype=jnp.int32)
    earlier = order[None, :] < order[:, None]
    matches = labels[:, None] == labels[None, :]
    block_rank = jnp.sum(jnp.logical_and(matches, earlier).astype(jnp.int32), axis=1)
    slot_of_block = labels * capacity + block_rank
    slot_match = slot_of_block[None, :] == jnp.arange(slot_total, dtype=jnp.int32)[:, None]
    source_block = jnp.sum(jnp.where(slot_match, order[None, :], 0), axis=1)
    occupied = jnp.any(slot_match, axis=1)

    def dispatch(rows_lo):
        blocks = rows_lo.reshape(blocks_dev, block, width)
        picked = jnp.take(blocks, source_block, axis=0)
        filled = jnp.where(occupied[:, None, None], picked, jnp.zeros((), rows_lo.dtype))
        outgoing = filled.reshape(experts, capacity * block, width)
        arrived = lax.all_to_all(outgoing, "expert", split_axis=0, concat_axis=0, tiled=True)
        return arrived.reshape(-1, width)

    def bring_home(partial_value):
        shaped = partial_value.reshape(experts, capacity * block, width)
        returned = lax.all_to_all(
            shaped.astype(jnp.bfloat16), "expert", split_axis=0, concat_axis=0, tiled=True
        ).astype(shaped.dtype)
        mine = jnp.take(returned.reshape(slot_total, block, width), slot_of_block, axis=0)
        result = lax.psum(mine.reshape(tok_rows, width).astype(jnp.bfloat16), "mp").astype(
            jnp.float32
        )
        return result

    up_matrix = weight_up[0]
    down_matrix = weight_down[0]
    contract_last = (((1,), (1,)), ((), ()))
    contract_first = (((0,), (0,)), ((), ()))
    routed_lo = dispatch(tokens.astype(jnp.bfloat16))
    pre_act = jnp.dot(routed_lo, up_matrix, preferred_element_type=jnp.float32)
    hidden = jax.nn.gelu(pre_act).astype(jnp.bfloat16)
    mixed_part = jnp.dot(hidden, down_matrix, preferred_element_type=jnp.float32)
    layer_output = tokens + bring_home(mixed_part)
    routed_up = dispatch(upstream.astype(jnp.bfloat16))
    hidden_grad = lax.dot_general(
        routed_up, down_matrix, contract_last, preferred_element_type=jnp.float32
    )
    unused, gelu_back = jax.vjp(jax.nn.gelu, pre_act)
    pre_grad = gelu_back(hidden_grad)[0].astype(jnp.bfloat16)
    token_part = lax.dot_general(
        pre_grad, up_matrix, contract_last, preferred_element_type=jnp.float32
    )
    up_part = lax.dot_general(
        routed_lo, pre_grad, contract_first, preferred_element_type=jnp.float32
    )
    down_part = lax.dot_general(
        hidden, routed_up, contract_first, preferred_element_type=jnp.float32
    )
    grad_tokens = upstream + bring_home(token_part)
    grad_up, grad_down = (
        lax.psum_scatter(
            up_part[None].astype(jnp.bfloat16), "dp", scatter_dimension=1, tiled=True
        ).astype(jnp.float32),
        lax.psum_scatter(
            down_part[None].astype(jnp.bfloat16), "dp", scatter_dimension=2, tiled=True
        ).astype(jnp.float32),
    )
    return (layer_output, grad_tokens, grad_up, grad_down)


def solution(mesh):
    placed = (
        P(("dp", "expert"), None),
        P(("dp", "expert"), None),
        P("expert", None, "mp"),
        P("expert", "mp", None),
        P(("dp", "expert"), None),
    )

    def body(tokens, block_experts, weight_up, weight_down, upstream):
        tok_rows, width = tokens.shape
        blocks_dev = block_experts.shape[0]
        fits = (
            (mesh.shape["dp"], mesh.shape["expert"], mesh.shape["mp"]) == (4, 4, 2)
            and blocks_dev % 2 == 0
            and (tok_rows // 4) % 16 == 0
            and width % (4 * TILE) == 0
            and weight_up.shape[2] % TILE == 0
        )
        chosen = fused_body if fits else plain_body
        return chosen(tokens, block_experts, weight_up, weight_down, upstream)

    return jax.shard_map(
        body,
        mesh=mesh,
        in_specs=placed,
        out_specs=(
            P(("dp", "expert"), None),
            P(("dp", "expert"), None),
            P("expert", "dp", "mp"),
            P("expert", "mp", "dp"),
        ),
        check_vma=False,
    )
```

```python
import jax
import jax.numpy as jnp
from jax import lax
from jax.experimental import pallas as pl
from jax.experimental.pallas import tpu as pltpu
from jax.sharding import PartitionSpec as P

MESH = pl.DeviceIdType.MESH
LAST = (((1,), (1,)), ((), ()))
FIRST = (((0,), (0,)), ((), ()))
F32 = jnp.float32
BF16 = jnp.bfloat16
TILE = 256
GRANT = 57 * 1024 * 1024


def flip(index, k):
    if k == 0:
        return index
    if k == 1:
        return index + 1 - 2 * lax.rem(index, 2)
    if k == 2:
        return lax.rem(index + 2, 4)
    return 3 - index


def remote(src, dst, send_sem, recv_sem, device):
    return pltpu.make_async_remote_copy(
        src_ref=src, dst_ref=dst, send_sem=send_sem, recv_sem=recv_sem, device_id=device, device_id_type=MESH
    )


def finish(*refs):
    sources, results, held = refs[:4], refs[4:8], refs[8:12]
    in_sem, out_sem = refs[12:]
    loads, stores = [], []
    for src, dst, kept in zip(sources, results, held):
        half = src.shape[0] // 2
        for part in range(2):
            rows = pl.ds(part * half, half)
            index = len(loads)
            loads.append(pltpu.make_async_copy(src.at[rows], kept.at[rows], in_sem.at[index]))
            stores.append(pltpu.make_async_copy(kept.at[rows], dst.at[rows], out_sem.at[index]))
    for load in loads:
        load.start()
    for load, store in zip(loads, stores):
        load.wait()
        store.start()
    for store in stores:
        store.wait()


def kernel(
    labels,
    tokens_hbm,
    upstream_hbm,
    up_hbm,
    down_hbm,
    layer_out,
    grad_tokens_out,
    grad_up_out,
    grad_down_out,
    rows_in,
    up,
    down,
    routed,
    gathered,
    hidden,
    slope_kept,
    pre_grad,
    parts,
    parts_in,
    summed,
    returned,
    grad_up,
    grad_down,
    grad_down_turned,
    shares,
    load_sem,
    store_sem,
    z_send,
    z_recv,
    x_send,
    x_recv,
    y_send,
    y_recv,
    s_send,
    s_recv,
    p_send,
    p_recv,
    r_send,
    r_recv,
    h_send,
    h_recv,
):
    dp = lax.axis_index("dp")
    me = lax.axis_index("expert")
    core = lax.axis_index("mp")
    other = 1 - core
    tok_rows, width = rows_in.shape[1], rows_in.shape[2]
    blocks_dev = labels.shape[1]
    block = tok_rows // blocks_dev
    slots = routed.shape[1]
    half = slots // 2
    piece = half // 4
    share = grad_up.shape[0]
    units = up.shape[1]

    loads = [
        pltpu.make_async_copy(tokens_hbm, rows_in.at[0], load_sem.at[0]),
        pltpu.make_async_copy(upstream_hbm, rows_in.at[1], load_sem.at[1]),
        pltpu.make_async_copy(up_hbm, up, load_sem.at[2]),
        pltpu.make_async_copy(down_hbm, down, load_sem.at[3]),
    ]
    for load in loads:
        load.start()

    x_peer = {"dp": flip(dp, 1)}
    y_peer = {"dp": flip(dp, 2)}
    sibling = {"mp": other}
    z_peers = [{"expert": flip(me, k)} for k in range(4)]
    barrier = pltpu.get_barrier_semaphore()
    for peer in z_peers[1:] + [x_peer, y_peer, sibling]:
        pl.semaphore_signal(barrier, inc=1, device_id=peer, device_id_type=MESH)

    experts_at = lax.broadcasted_iota(jnp.int32, (128, blocks_dev), 0)
    named = (labels[...] == experts_at).astype(F32)
    row_at = lax.broadcasted_iota(jnp.int32, (tok_rows, blocks_dev), 0)
    first_row = lax.broadcasted_iota(jnp.int32, (tok_rows, blocks_dev), 1) * block
    in_block = jnp.logical_and(row_at >= first_row, row_at < first_row + block)
    before = row_at >= first_row + block
    row_expert = lax.dot_general(in_block.astype(F32), named, LAST, preferred_element_type=F32)
    row_rank = lax.dot_general(before.astype(F32), named, LAST, preferred_element_type=F32)
    start = lax.broadcasted_iota(jnp.int32, (tok_rows, 128), 1).astype(F32) * piece
    first_slot = jnp.sum(row_expert * start, axis=1, keepdims=True)
    place = jnp.sum(row_expert * (block * row_rank), axis=1, keepdims=True)
    place += jnp.sum(jnp.where(in_block, row_at - first_row, 0).astype(F32), axis=1, keepdims=True)
    slot_of_row = first_slot + place + jnp.where(place >= piece, float(half - piece), 0.0)
    slot_at = lax.broadcasted_iota(jnp.int32, (tok_rows, slots), 1).astype(F32)
    picks = (slot_of_row == slot_at).astype(BF16)

    def one(side, k):
        return pl.ds(pl.multiple_of(side * half + flip(me, k) * piece, piece), piece)

    def pair(side, p):
        q = lax.div(me, 2)
        at = q if p == 0 else 1 - q
        return pl.ds(pl.multiple_of(side * half + at * (2 * piece), 2 * piece), 2 * piece)

    sent = []

    def go(src, dst, send_sem, recv_sem, peer):
        copy = remote(src, dst, send_sem, recv_sem, peer)
        copy.start()
        sent.append(copy)

    def arrived(dst, send_sem, recv_sem, peer):
        remote(dst, dst, send_sem, recv_sem, peer).wait_recv()

    def route(a):
        loads[a].wait()
        rows_lo = rows_in[a].astype(BF16)
        routed[a] = lax.dot_general(picks, rows_lo, FIRST, preferred_element_type=F32).astype(BF16)

    def dispatch(a, k):
        go(
            routed.at[a, one(core, k)],
            gathered.at[a, dp, one(core, 0)],
            z_send.at[a, k],
            z_recv.at[a, k],
            z_peers[k],
        )

    def keep_own(a):
        gathered[a, dp, one(core, 0), :] = routed[a, one(core, 0), :]

    def block_at(a, rel, p, side=None):
        return gathered.at[a, flip(dp, rel), pair(core if side is None else side, p)]

    def to_sibling(a, rel, p):
        go(block_at(a, rel, p), block_at(a, rel, p), s_send.at[a, rel, p], s_recv.at[a, rel, p], sibling)

    def from_sibling(a, rel):
        for p in range(2):
            arrived(block_at(a, rel, p, other), s_send.at[a, rel, p], s_recv.at[a, rel, p], sibling)

    def push(rows, a, unit):
        go(gathered.at[a, dp, rows], gathered.at[a, dp, rows], x_send.at[a, unit], x_recv.at[a, unit], x_peer)
        go(gathered.at[a, dp, rows], gathered.at[a, dp, rows], y_send.at[a, unit], y_recv.at[a, unit], y_peer)

    def spread(a, p):
        for k in (2 * p, 2 * p + 1):
            if k:
                arrived(gathered.at[a, dp, one(core, k)], z_send.at[a, k], z_recv.at[a, k], z_peers[k])
                if a == 0:
                    dispatch(1, k)
        to_sibling(a, 0, p)
        if p == 0:
            push(one(core, 1), a, 1)
        else:
            push(pair(core, 1), a, 2)

    def units_arrived(a, rel, p, send, recv, peer):
        held = gathered.at[a, flip(dp, rel)]
        if p == 0:
            for k in range(2):
                arrived(held.at[one(core, k)], send.at[a, k], recv.at[a, k], peer)
        else:
            arrived(held.at[pair(core, 1)], send.at[a, 2], recv.at[a, 2], peer)

    def pass_on(a, p):
        units_arrived(a, 1, p, x_send, x_recv, x_peer)
        if p == 0:
            go(block_at(a, 1, 0), block_at(a, 1, 0), y_send.at[a, 3], y_recv.at[a, 3], y_peer)
        to_sibling(a, 1, p)
        units_arrived(a, 2, p, y_send, y_recv, y_peer)
        if p == 1:
            go(block_at(a, 2, 1), block_at(a, 2, 1), x_send.at[a, 3], x_recv.at[a, 3], x_peer)
        to_sibling(a, 2, p)

    def from_corner(a):
        arrived(block_at(a, 3, 0), y_send.at[a, 3], y_recv.at[a, 3], y_peer)
        to_sibling(a, 3, 0)
        arrived(block_at(a, 3, 1), x_send.at[a, 3], x_recv.at[a, 3], x_peer)
        to_sibling(a, 3, 1)

    mine_cols = pl.ds(pl.multiple_of(dp * share, share), share)

    def activation(value):
        scale = 0.7978845608028654
        square = value * value
        turn = jnp.tanh(value * (scale + (scale * 0.044715) * square))
        cdf = 0.5 + 0.5 * turn
        slope = cdf + value * (0.5 - 0.5 * turn * turn) * (scale + (3 * scale * 0.044715) * square)
        return (value * cdf).astype(BF16), slope

    def tiles(total, step):
        for index in range(total // TILE):
            step(pl.ds(index * TILE, TILE))

    def forward(rel):
        at = flip(dp, rel)

        def step(cols):
            value = jnp.dot(gathered[0, at], up[:, cols], preferred_element_type=F32)
            hidden[rel, :, cols], slope_kept[rel, :, cols] = activation(value)

        tiles(units, step)

    def backward(rel):
        at = flip(dp, rel)

        def step(cols):
            back = lax.dot_general(gathered[1, at], down[cols, :], LAST, preferred_element_type=F32)
            pre_grad[rel, :, cols] = (back * slope_kept[rel, :, cols]).astype(BF16)

        tiles(units, step)

    def mix(cols):
        parts[0, :, cols] = jnp.dot(hidden[0], down[:, cols], preferred_element_type=F32).astype(BF16)

    def unmix(cols):
        parts[1, :, cols] = lax.dot_general(
            pre_grad[0], up[cols, :], LAST, preferred_element_type=F32
        ).astype(BF16)

    def add_grads(rel):
        for a in range(2):
            shares[a] = gathered[a, flip(dp, rel), :, mine_cols].T

        def step(cols):
            part_up = jnp.dot(shares[0], pre_grad[rel, :, cols], preferred_element_type=F32)
            part_down = jnp.dot(shares[1], hidden[rel, :, cols], preferred_element_type=F32)
            if rel == 0:
                grad_up[:, cols] = part_up
                grad_down_turned[:, cols] = part_down
            else:
                grad_up[:, cols] += part_up
                grad_down_turned[:, cols] += part_down

        tiles(units, step)

    def turn_down(cols):
        grad_down[cols, :] = grad_down_turned[:, cols].T

    def swap(a):
        theirs = pl.ds(pl.multiple_of(other * half, half), half)
        go(parts.at[a, theirs], parts_in.at[a], p_send.at[a], p_recv.at[a], sibling)

    def send_home(a):
        arrived(parts_in.at[a], p_send.at[a], p_recv.at[a], sibling)
        ours = pl.ds(pl.multiple_of(core * half, half), half)
        summed[a] = (parts[a, ours, :].astype(F32) + parts_in[a].astype(F32)).astype(BF16)
        for k in (2, 3, 1):
            go(
                summed.at[a, pl.ds(pl.multiple_of(flip(me, k) * piece, piece), piece)],
                returned.at[a, one(core, 0)],
                r_send.at[a, k],
                r_recv.at[a, k],
                z_peers[k],
            )
        returned[a, one(core, 0), :] = summed[a, pl.ds(pl.multiple_of(me * piece, piece), piece), :]

    def reach_home(a, p):
        for k in (2 * p, 2 * p + 1):
            if k:
                arrived(returned.at[a, one(core, k)], r_send.at[a, k], r_recv.at[a, k], z_peers[k])
        block = returned.at[a, pair(core, p)]
        go(block, block, h_send.at[a, p], h_recv.at[a, p], sibling)

    stores = []

    def store(src, dst):
        copy = pltpu.make_async_copy(src, dst, store_sem.at[len(stores)])
        copy.start()
        stores.append(copy)

    def add_home(a, out):
        for p in range(2):
            arrived(returned.at[a, pair(other, p)], h_send.at[a, p], h_recv.at[a, p], sibling)
        rows_in[a] += jnp.dot(picks, returned[a], preferred_element_type=F32)
        store(rows_in.at[a], out)

    route(0)
    pl.semaphore_wait(barrier, 6)
    for k in (1, 2, 3):
        dispatch(0, k)
    keep_own(0)
    push(one(core, 0), 0, 0)
    route(1)
    keep_own(1)
    push(one(core, 0), 1, 0)
    spread(0, 0)
    pass_on(0, 0)
    spread(0, 1)
    spread(1, 0)
    loads[2].wait()
    loads[3].wait()
    from_sibling(0, 0)
    forward(0)
    tiles(width, mix)
    swap(0)
    pass_on(0, 1)
    send_home(0)
    pass_on(1, 0)
    spread(1, 1)
    from_sibling(0, 1)
    forward(1)
    from_sibling(1, 0)
    backward(0)
    tiles(width, unmix)
    swap(1)
    pass_on(1, 1)
    add_grads(0)
    send_home(1)
    from_corner(0)
    from_sibling(0, 2)
    forward(2)
    from_sibling(1, 1)
    backward(1)
    add_grads(1)
    from_corner(1)
    from_sibling(0, 3)
    forward(3)
    from_sibling(1, 2)
    backward(2)
    add_grads(2)
    reach_home(0, 0)
    reach_home(0, 1)
    from_sibling(1, 3)
    backward(3)
    add_grads(3)
    store(grad_up, grad_up_out)
    tiles(units, turn_down)
    store(grad_down, grad_down_out)
    reach_home(1, 0)
    add_home(0, layer_out)
    reach_home(1, 1)
    add_home(1, grad_tokens_out)
    for copy in sent:
        copy.wait_send()
    for copy in stores:
        copy.wait()


def fused_body(tokens, block_experts, weight_up, weight_down, upstream):
    tok_rows, width = tokens.shape
    blocks_dev = block_experts.shape[0]
    units = weight_up.shape[2]
    slots = 2 * tok_rows
    half = slots // 2
    share = width // 4
    in_hbm = pl.BlockSpec(memory_space=pltpu.HBM)
    anywhere = pl.BlockSpec(memory_space=pl.ANY)
    flops = 2 * slots * width * units * 12
    results = (
        jax.ShapeDtypeStruct((tok_rows, width), F32),
        jax.ShapeDtypeStruct((tok_rows, width), F32),
        jax.ShapeDtypeStruct((share, units), F32),
        jax.ShapeDtypeStruct((units, share), F32),
    )
    held = pl.pallas_call(
        kernel,
        out_shape=results,
        in_specs=[pl.BlockSpec(memory_space=pltpu.VMEM)] + [in_hbm] * 4,
        out_specs=(anywhere,) * 4,
        scratch_shapes=[
            pltpu.VMEM((2, tok_rows, width), F32),
            pltpu.VMEM((width, units), BF16),
            pltpu.VMEM((units, width), BF16),
            pltpu.VMEM((2, slots, width), BF16),
            pltpu.VMEM((2, 4, slots, width), BF16),
            pltpu.VMEM((4, slots, units), BF16),
            pltpu.VMEM((4, slots, units), F32),
            pltpu.VMEM((4, slots, units), BF16),
            pltpu.VMEM((2, slots, width), BF16),
            pltpu.VMEM((2, half, width), BF16),
            pltpu.VMEM((2, half, width), BF16),
            pltpu.VMEM((2, slots, width), BF16),
            pltpu.VMEM((share, units), F32),
            pltpu.VMEM((units, share), F32),
            pltpu.VMEM((share, units), F32),
            pltpu.VMEM((2, share, slots), BF16),
            pltpu.SemaphoreType.DMA((4,)),
            pltpu.SemaphoreType.DMA((4,)),
            pltpu.SemaphoreType.DMA((2, 4)),
            pltpu.SemaphoreType.DMA((2, 4)),
            pltpu.SemaphoreType.DMA((2, 4)),
            pltpu.SemaphoreType.DMA((2, 4)),
            pltpu.SemaphoreType.DMA((2, 4)),
            pltpu.SemaphoreType.DMA((2, 4)),
            pltpu.SemaphoreType.DMA((2, 4, 2)),
            pltpu.SemaphoreType.DMA((2, 4, 2)),
            pltpu.SemaphoreType.DMA((2,)),
            pltpu.SemaphoreType.DMA((2,)),
            pltpu.SemaphoreType.DMA((2, 4)),
            pltpu.SemaphoreType.DMA((2, 4)),
            pltpu.SemaphoreType.DMA((2, 2)),
            pltpu.SemaphoreType.DMA((2, 2)),
        ],
        compiler_params=pltpu.CompilerParams(
            collective_id=0, has_side_effects=True, vmem_limit_bytes=GRANT
        ),
        cost_estimate=pl.CostEstimate(flops=flops, bytes_accessed=8 << 20, transcendentals=slots * units * 4),
    )(block_experts.reshape(1, blocks_dev), tokens, upstream, weight_up[0], weight_down[0])
    layer_output, grad_tokens, grad_up, grad_down = pl.pallas_call(
        finish,
        out_shape=results,
        in_specs=[anywhere] * 4,
        out_specs=(in_hbm,) * 4,
        scratch_shapes=[pltpu.VMEM(result.shape, F32) for result in results]
        + [pltpu.SemaphoreType.DMA((8,)), pltpu.SemaphoreType.DMA((8,))],
        compiler_params=pltpu.CompilerParams(vmem_limit_bytes=GRANT),
        cost_estimate=pl.CostEstimate(flops=0, bytes_accessed=3 << 20, transcendentals=0),
    )(*held)
    return layer_output, grad_tokens, grad_up[None], grad_down[None]


def plain_body(tokens, block_experts, weight_up, weight_down, upstream):
    experts = lax.axis_size("expert")
    blocks_dev = block_experts.shape[0]
    tok_rows = tokens.shape[0]
    width = tokens.shape[1]
    block = tok_rows // blocks_dev
    capacity = max(1, blocks_dev * 2 // experts)
    slot_total = experts * capacity
    labels = block_experts[:, 0]
    order = jnp.arange(blocks_dev, dtype=jnp.int32)
    earlier = order[None, :] < order[:, None]
    matches = labels[:, None] == labels[None, :]
    block_rank = jnp.sum(jnp.logical_and(matches, earlier).astype(jnp.int32), axis=1)
    slot_of_block = labels * capacity + block_rank
    slot_match = slot_of_block[None, :] == jnp.arange(slot_total, dtype=jnp.int32)[:, None]
    source_block = jnp.sum(jnp.where(slot_match, order[None, :], 0), axis=1)
    occupied = jnp.any(slot_match, axis=1)

    def dispatch(rows_lo):
        blocks = rows_lo.reshape(blocks_dev, block, width)
        picked = jnp.take(blocks, source_block, axis=0)
        filled = jnp.where(occupied[:, None, None], picked, jnp.zeros((), rows_lo.dtype))
        outgoing = filled.reshape(experts, capacity * block, width)
        arrived = lax.all_to_all(outgoing, "expert", split_axis=0, concat_axis=0, tiled=True)
        return arrived.reshape(-1, width)

    def bring_home(partial_value):
        shaped = partial_value.reshape(experts, capacity * block, width)
        returned = lax.all_to_all(
            shaped.astype(jnp.bfloat16), "expert", split_axis=0, concat_axis=0, tiled=True
        ).astype(shaped.dtype)
        mine = jnp.take(returned.reshape(slot_total, block, width), slot_of_block, axis=0)
        result = lax.psum(mine.reshape(tok_rows, width).astype(jnp.bfloat16), "mp").astype(
            jnp.float32
        )
        return result

    up_matrix = weight_up[0]
    down_matrix = weight_down[0]
    contract_last = (((1,), (1,)), ((), ()))
    contract_first = (((0,), (0,)), ((), ()))
    routed_lo = dispatch(tokens.astype(jnp.bfloat16))
    pre_act = jnp.dot(routed_lo, up_matrix, preferred_element_type=jnp.float32)
    hidden = jax.nn.gelu(pre_act).astype(jnp.bfloat16)
    mixed_part = jnp.dot(hidden, down_matrix, preferred_element_type=jnp.float32)
    layer_output = tokens + bring_home(mixed_part)
    routed_up = dispatch(upstream.astype(jnp.bfloat16))
    hidden_grad = lax.dot_general(
        routed_up, down_matrix, contract_last, preferred_element_type=jnp.float32
    )
    unused, gelu_back = jax.vjp(jax.nn.gelu, pre_act)
    pre_grad = gelu_back(hidden_grad)[0].astype(jnp.bfloat16)
    token_part = lax.dot_general(
        pre_grad, up_matrix, contract_last, preferred_element_type=jnp.float32
    )
    up_part = lax.dot_general(
        routed_lo, pre_grad, contract_first, preferred_element_type=jnp.float32
    )
    down_part = lax.dot_general(
        hidden, routed_up, contract_first, preferred_element_type=jnp.float32
    )
    grad_tokens = upstream + bring_home(token_part)
    grad_up, grad_down = (
        lax.psum_scatter(
            up_part[None].astype(jnp.bfloat16), "dp", scatter_dimension=1, tiled=True
        ).astype(jnp.float32),
        lax.psum_scatter(
            down_part[None].astype(jnp.bfloat16), "dp", scatter_dimension=2, tiled=True
        ).astype(jnp.float32),
    )
    return (layer_output, grad_tokens, grad_up, grad_down)


def solution(mesh):
    placed = (
        P(("dp", "expert"), None),
        P(("dp", "expert"), None),
        P("expert", None, "mp"),
        P("expert", "mp", None),
        P(("dp", "expert"), None),
    )

    def body(tokens, block_experts, weight_up, weight_down, upstream):
        tok_rows, width = tokens.shape
        blocks_dev = block_experts.shape[0]
        fits = (
            (mesh.shape["dp"], mesh.shape["expert"], mesh.shape["mp"]) == (4, 4, 2)
            and blocks_dev % 2 == 0
            and (tok_rows // 4) % 16 == 0
            and width % (4 * TILE) == 0
            and weight_up.shape[2] % TILE == 0
        )
        chosen = fused_body if fits else plain_body
        return chosen(tokens, block_experts, weight_up, weight_down, upstream)

    return jax.shard_map(
        body,
        mesh=mesh,
        in_specs=placed,
        out_specs=(
            P(("dp", "expert"), None),
            P(("dp", "expert"), None),
            P("expert", "dp", "mp"),
            P("expert", "mp", "dp"),
        ),
        check_vma=False,
    )
```

```python
import jax
import jax.numpy as jnp
from jax import lax
from jax.experimental import pallas as pl
from jax.experimental.pallas import tpu as pltpu
from jax.sharding import PartitionSpec as P

MESH = pl.DeviceIdType.MESH
LAST = (((1,), (1,)), ((), ()))
FIRST = (((0,), (0,)), ((), ()))
F32 = jnp.float32
BF16 = jnp.bfloat16
TILE = 256
GRANT = 57 * 1024 * 1024


def flip(index, k):
    if k == 0:
        return index
    if k == 1:
        return index + 1 - 2 * lax.rem(index, 2)
    if k == 2:
        return lax.rem(index + 2, 4)
    return 3 - index


def remote(src, dst, send_sem, recv_sem, device):
    return pltpu.make_async_remote_copy(
        src_ref=src, dst_ref=dst, send_sem=send_sem, recv_sem=recv_sem, device_id=device, device_id_type=MESH
    )


def finish(*refs):
    sources, results, held = refs[:4], refs[4:8], refs[8:12]
    in_sem, out_sem = refs[12:]
    loads, stores = [], []
    for src, dst, kept in zip(sources, results, held):
        half = src.shape[0] // 2
        for part in range(2):
            rows = pl.ds(part * half, half)
            index = len(loads)
            loads.append(pltpu.make_async_copy(src.at[rows], kept.at[rows], in_sem.at[index]))
            stores.append(pltpu.make_async_copy(kept.at[rows], dst.at[rows], out_sem.at[index]))
    for load in loads:
        load.start()
    for load, store in zip(loads, stores):
        load.wait()
        store.start()
    for store in stores:
        store.wait()


def kernel(
    labels,
    tokens_hbm,
    upstream_hbm,
    up_hbm,
    down_hbm,
    layer_out,
    grad_tokens_out,
    grad_up_out,
    grad_down_out,
    rows_in,
    up,
    down,
    routed,
    gathered,
    hidden,
    slope_kept,
    pre_grad,
    parts,
    parts_in,
    summed,
    returned,
    grad_up,
    grad_down,
    grad_down_turned,
    shares,
    load_sem,
    store_sem,
    z_send,
    z_recv,
    x_send,
    x_recv,
    y_send,
    y_recv,
    s_send,
    s_recv,
    p_send,
    p_recv,
    r_send,
    r_recv,
    h_send,
    h_recv,
):
    dp = lax.axis_index("dp")
    me = lax.axis_index("expert")
    core = lax.axis_index("mp")
    other = 1 - core
    tok_rows, width = rows_in.shape[1], rows_in.shape[2]
    blocks_dev = labels.shape[1]
    block = tok_rows // blocks_dev
    slots = routed.shape[1]
    half = slots // 2
    piece = half // 4
    share = grad_up.shape[0]
    units = up.shape[1]

    loads = [
        pltpu.make_async_copy(tokens_hbm, rows_in.at[0], load_sem.at[0]),
        pltpu.make_async_copy(upstream_hbm, rows_in.at[1], load_sem.at[1]),
        pltpu.make_async_copy(up_hbm, up, load_sem.at[2]),
        pltpu.make_async_copy(down_hbm, down, load_sem.at[3]),
    ]
    for load in loads:
        load.start()

    x_peer = {"dp": flip(dp, 1)}
    y_peer = {"dp": flip(dp, 2)}
    sibling = {"mp": other}
    z_peers = [{"expert": flip(me, k)} for k in range(4)]
    barrier = pltpu.get_barrier_semaphore()
    for peer in z_peers[1:] + [x_peer, y_peer, sibling]:
        pl.semaphore_signal(barrier, inc=1, device_id=peer, device_id_type=MESH)

    experts_at = lax.broadcasted_iota(jnp.int32, (128, blocks_dev), 0)
    named = (labels[...] == experts_at).astype(F32)
    row_at = lax.broadcasted_iota(jnp.int32, (tok_rows, blocks_dev), 0)
    first_row = lax.broadcasted_iota(jnp.int32, (tok_rows, blocks_dev), 1) * block
    in_block = jnp.logical_and(row_at >= first_row, row_at < first_row + block)
    before = row_at >= first_row + block
    row_expert = lax.dot_general(in_block.astype(F32), named, LAST, preferred_element_type=F32)
    row_rank = lax.dot_general(before.astype(F32), named, LAST, preferred_element_type=F32)
    start = lax.broadcasted_iota(jnp.int32, (tok_rows, 128), 1).astype(F32) * piece
    first_slot = jnp.sum(row_expert * start, axis=1, keepdims=True)
    place = jnp.sum(row_expert * (block * row_rank), axis=1, keepdims=True)
    place += jnp.sum(jnp.where(in_block, row_at - first_row, 0).astype(F32), axis=1, keepdims=True)
    slot_of_row = first_slot + place + jnp.where(place >= piece, float(half - piece), 0.0)
    slot_at = lax.broadcasted_iota(jnp.int32, (tok_rows, slots), 1).astype(F32)
    picks = (slot_of_row == slot_at).astype(BF16)

    def one(side, k):
        return pl.ds(pl.multiple_of(side * half + flip(me, k) * piece, piece), piece)

    def pair(side, p):
        q = lax.div(me, 2)
        at = q if p == 0 else 1 - q
        return pl.ds(pl.multiple_of(side * half + at * (2 * piece), 2 * piece), 2 * piece)

    sent = []

    def go(src, dst, send_sem, recv_sem, peer):
        copy = remote(src, dst, send_sem, recv_sem, peer)
        copy.start()
        sent.append(copy)

    def arrived(dst, send_sem, recv_sem, peer):
        remote(dst, dst, send_sem, recv_sem, peer).wait_recv()

    def route(a):
        loads[a].wait()
        rows_lo = rows_in[a].astype(BF16)
        routed[a] = lax.dot_general(picks, rows_lo, FIRST, preferred_element_type=F32).astype(BF16)

    def dispatch(a, k):
        go(
            routed.at[a, one(core, k)],
            gathered.at[a, dp, one(core, 0)],
            z_send.at[a, k],
            z_recv.at[a, k],
            z_peers[k],
        )

    def keep_own(a):
        gathered[a, dp, one(core, 0), :] = routed[a, one(core, 0), :]

    def block_at(a, rel, p, side=None):
        return gathered.at[a, flip(dp, rel), pair(core if side is None else side, p)]

    def to_sibling(a, rel, p):
        go(block_at(a, rel, p), block_at(a, rel, p), s_send.at[a, rel, p], s_recv.at[a, rel, p], sibling)

    def from_sibling(a, rel):
        for p in range(2):
            arrived(block_at(a, rel, p, other), s_send.at[a, rel, p], s_recv.at[a, rel, p], sibling)

    def push(rows, a, unit):
        go(gathered.at[a, dp, rows], gathered.at[a, dp, rows], x_send.at[a, unit], x_recv.at[a, unit], x_peer)
        go(gathered.at[a, dp, rows], gathered.at[a, dp, rows], y_send.at[a, unit], y_recv.at[a, unit], y_peer)

    def spread(a, p):
        for k in (2 * p, 2 * p + 1):
            if k:
                arrived(gathered.at[a, dp, one(core, k)], z_send.at[a, k], z_recv.at[a, k], z_peers[k])
                if a == 0:
                    dispatch(1, k)
        to_sibling(a, 0, p)
        if p == 0:
            push(one(core, 1), a, 1)
        else:
            push(pair(core, 1), a, 2)

    def units_arrived(a, rel, p, send, recv, peer):
        held = gathered.at[a, flip(dp, rel)]
        if p == 0:
            for k in range(2):
                arrived(held.at[one(core, k)], send.at[a, k], recv.at[a, k], peer)
        else:
            arrived(held.at[pair(core, 1)], send.at[a, 2], recv.at[a, 2], peer)

    def pass_on(a, p):
        units_arrived(a, 1, p, x_send, x_recv, x_peer)
        if p == 0:
            go(block_at(a, 1, 0), block_at(a, 1, 0), y_send.at[a, 3], y_recv.at[a, 3], y_peer)
        to_sibling(a, 1, p)
        units_arrived(a, 2, p, y_send, y_recv, y_peer)
        if p == 1:
            go(block_at(a, 2, 1), block_at(a, 2, 1), x_send.at[a, 3], x_recv.at[a, 3], x_peer)
        to_sibling(a, 2, p)

    def from_corner(a):
        arrived(block_at(a, 3, 0), y_send.at[a, 3], y_recv.at[a, 3], y_peer)
        to_sibling(a, 3, 0)
        arrived(block_at(a, 3, 1), x_send.at[a, 3], x_recv.at[a, 3], x_peer)
        to_sibling(a, 3, 1)

    mine_cols = pl.ds(pl.multiple_of(dp * share, share), share)

    def activation(value):
        scale = 0.7978845608028654
        square = value * value
        turn = jnp.tanh(value * (scale + (scale * 0.044715) * square))
        cdf = 0.5 + 0.5 * turn
        slope = cdf + value * (0.5 - 0.5 * turn * turn) * (scale + (3 * scale * 0.044715) * square)
        return (value * cdf).astype(BF16), slope

    def tiles(total, step):
        for index in range(total // TILE):
            step(pl.ds(index * TILE, TILE))

    def forward(rel):
        at = flip(dp, rel)

        def step(cols):
            value = jnp.dot(gathered[0, at], up[:, cols], preferred_element_type=F32)
            hidden[rel, :, cols], slope_kept[rel, :, cols] = activation(value)

        tiles(units, step)

    def backward(rel):
        at = flip(dp, rel)

        def step(cols):
            back = lax.dot_general(gathered[1, at], down[cols, :], LAST, preferred_element_type=F32)
            pre_grad[rel, :, cols] = (back * slope_kept[rel, :, cols]).astype(BF16)

        tiles(units, step)

    def mix(cols):
        parts[0, :, cols] = jnp.dot(hidden[0], down[:, cols], preferred_element_type=F32).astype(BF16)

    def unmix(cols):
        parts[1, :, cols] = lax.dot_general(
            pre_grad[0], up[cols, :], LAST, preferred_element_type=F32
        ).astype(BF16)

    def add_grads(rel):
        for a in range(2):
            shares[a] = gathered[a, flip(dp, rel), :, mine_cols].T

        def step(cols):
            part_up = jnp.dot(shares[0], pre_grad[rel, :, cols], preferred_element_type=F32)
            part_down = jnp.dot(shares[1], hidden[rel, :, cols], preferred_element_type=F32)
            if rel == 0:
                grad_up[:, cols] = part_up
                grad_down_turned[:, cols] = part_down
            else:
                grad_up[:, cols] += part_up
                grad_down_turned[:, cols] += part_down

        tiles(units, step)

    def turn_down(cols):
        grad_down[cols, :] = grad_down_turned[:, cols].T

    def swap(a):
        theirs = pl.ds(pl.multiple_of(other * half, half), half)
        go(parts.at[a, theirs], parts_in.at[a], p_send.at[a], p_recv.at[a], sibling)

    def send_home(a):
        arrived(parts_in.at[a], p_send.at[a], p_recv.at[a], sibling)
        ours = pl.ds(pl.multiple_of(core * half, half), half)
        summed[a] = (parts[a, ours, :].astype(F32) + parts_in[a].astype(F32)).astype(BF16)
        for k in (2, 3, 1):
            go(
                summed.at[a, pl.ds(pl.multiple_of(flip(me, k) * piece, piece), piece)],
                returned.at[a, one(core, 0)],
                r_send.at[a, k],
                r_recv.at[a, k],
                z_peers[k],
            )
        returned[a, one(core, 0), :] = summed[a, pl.ds(pl.multiple_of(me * piece, piece), piece), :]

    def reach_home(a, p):
        for k in (2 * p, 2 * p + 1):
            if k:
                arrived(returned.at[a, one(core, k)], r_send.at[a, k], r_recv.at[a, k], z_peers[k])
        block = returned.at[a, pair(core, p)]
        go(block, block, h_send.at[a, p], h_recv.at[a, p], sibling)

    stores = []

    def store(src, dst):
        copy = pltpu.make_async_copy(src, dst, store_sem.at[len(stores)])
        copy.start()
        stores.append(copy)

    def add_home(a, out):
        for p in range(2):
            arrived(returned.at[a, pair(other, p)], h_send.at[a, p], h_recv.at[a, p], sibling)
        rows_in[a] += jnp.dot(picks, returned[a], preferred_element_type=F32)
        store(rows_in.at[a], out)

    route(0)
    pl.semaphore_wait(barrier, 6)
    for k in (1, 2, 3):
        dispatch(0, k)
    keep_own(0)
    push(one(core, 0), 0, 0)
    route(1)
    keep_own(1)
    push(one(core, 0), 1, 0)
    spread(0, 0)
    pass_on(0, 0)
    spread(0, 1)
    spread(1, 0)
    loads[2].wait()
    loads[3].wait()
    from_sibling(0, 0)
    forward(0)
    tiles(width, mix)
    swap(0)
    pass_on(0, 1)
    send_home(0)
    pass_on(1, 0)
    spread(1, 1)
    from_sibling(0, 1)
    forward(1)
    from_sibling(1, 0)
    backward(0)
    tiles(width, unmix)
    swap(1)
    add_grads(0)
    pass_on(1, 1)
    send_home(1)
    from_corner(0)
    from_sibling(0, 2)
    forward(2)
    from_sibling(1, 1)
    backward(1)
    add_grads(1)
    from_sibling(0, 3)
    forward(3)
    from_corner(1)
    reach_home(0, 0)
    reach_home(0, 1)
    from_sibling(1, 2)
    backward(2)
    add_grads(2)
    add_home(0, layer_out)
    reach_home(1, 0)
    from_sibling(1, 3)
    backward(3)
    add_grads(3)
    store(grad_up, grad_up_out)
    reach_home(1, 1)
    tiles(units, turn_down)
    store(grad_down, grad_down_out)
    add_home(1, grad_tokens_out)
    for copy in sent:
        copy.wait_send()
    for copy in stores:
        copy.wait()


def fused_body(tokens, block_experts, weight_up, weight_down, upstream):
    tok_rows, width = tokens.shape
    blocks_dev = block_experts.shape[0]
    units = weight_up.shape[2]
    slots = 2 * tok_rows
    half = slots // 2
    share = width // 4
    in_hbm = pl.BlockSpec(memory_space=pltpu.HBM)
    anywhere = pl.BlockSpec(memory_space=pl.ANY)
    flops = 2 * slots * width * units * 12
    results = (
        jax.ShapeDtypeStruct((tok_rows, width), F32),
        jax.ShapeDtypeStruct((tok_rows, width), F32),
        jax.ShapeDtypeStruct((share, units), F32),
        jax.ShapeDtypeStruct((units, share), F32),
    )
    held = pl.pallas_call(
        kernel,
        out_shape=results,
        in_specs=[pl.BlockSpec(memory_space=pltpu.VMEM)] + [in_hbm] * 4,
        out_specs=(anywhere,) * 4,
        scratch_shapes=[
            pltpu.VMEM((2, tok_rows, width), F32),
            pltpu.VMEM((width, units), BF16),
            pltpu.VMEM((units, width), BF16),
            pltpu.VMEM((2, slots, width), BF16),
            pltpu.VMEM((2, 4, slots, width), BF16),
            pltpu.VMEM((4, slots, units), BF16),
            pltpu.VMEM((4, slots, units), F32),
            pltpu.VMEM((4, slots, units), BF16),
            pltpu.VMEM((2, slots, width), BF16),
            pltpu.VMEM((2, half, width), BF16),
            pltpu.VMEM((2, half, width), BF16),
            pltpu.VMEM((2, slots, width), BF16),
            pltpu.VMEM((share, units), F32),
            pltpu.VMEM((units, share), F32),
            pltpu.VMEM((share, units), F32),
            pltpu.VMEM((2, share, slots), BF16),
            pltpu.SemaphoreType.DMA((4,)),
            pltpu.SemaphoreType.DMA((4,)),
            pltpu.SemaphoreType.DMA((2, 4)),
            pltpu.SemaphoreType.DMA((2, 4)),
            pltpu.SemaphoreType.DMA((2, 4)),
            pltpu.SemaphoreType.DMA((2, 4)),
            pltpu.SemaphoreType.DMA((2, 4)),
            pltpu.SemaphoreType.DMA((2, 4)),
            pltpu.SemaphoreType.DMA((2, 4, 2)),
            pltpu.SemaphoreType.DMA((2, 4, 2)),
            pltpu.SemaphoreType.DMA((2,)),
            pltpu.SemaphoreType.DMA((2,)),
            pltpu.SemaphoreType.DMA((2, 4)),
            pltpu.SemaphoreType.DMA((2, 4)),
            pltpu.SemaphoreType.DMA((2, 2)),
            pltpu.SemaphoreType.DMA((2, 2)),
        ],
        compiler_params=pltpu.CompilerParams(
            collective_id=0, has_side_effects=True, vmem_limit_bytes=GRANT
        ),
        cost_estimate=pl.CostEstimate(flops=flops, bytes_accessed=8 << 20, transcendentals=slots * units * 4),
    )(block_experts.reshape(1, blocks_dev), tokens, upstream, weight_up[0], weight_down[0])
    layer_output, grad_tokens, grad_up, grad_down = pl.pallas_call(
        finish,
        out_shape=results,
        in_specs=[anywhere] * 4,
        out_specs=(in_hbm,) * 4,
        scratch_shapes=[pltpu.VMEM(result.shape, F32) for result in results]
        + [pltpu.SemaphoreType.DMA((8,)), pltpu.SemaphoreType.DMA((8,))],
        compiler_params=pltpu.CompilerParams(vmem_limit_bytes=GRANT),
        cost_estimate=pl.CostEstimate(flops=0, bytes_accessed=3 << 20, transcendentals=0),
    )(*held)
    return layer_output, grad_tokens, grad_up[None], grad_down[None]


def plain_body(tokens, block_experts, weight_up, weight_down, upstream):
    experts = lax.axis_size("expert")
    blocks_dev = block_experts.shape[0]
    tok_rows = tokens.shape[0]
    width = tokens.shape[1]
    block = tok_rows // blocks_dev
    capacity = max(1, blocks_dev * 2 // experts)
    slot_total = experts * capacity
    labels = block_experts[:, 0]
    order = jnp.arange(blocks_dev, dtype=jnp.int32)
    earlier = order[None, :] < order[:, None]
    matches = labels[:, None] == labels[None, :]
    block_rank = jnp.sum(jnp.logical_and(matches, earlier).astype(jnp.int32), axis=1)
    slot_of_block = labels * capacity + block_rank
    slot_match = slot_of_block[None, :] == jnp.arange(slot_total, dtype=jnp.int32)[:, None]
    source_block = jnp.sum(jnp.where(slot_match, order[None, :], 0), axis=1)
    occupied = jnp.any(slot_match, axis=1)

    def dispatch(rows_lo):
        blocks = rows_lo.reshape(blocks_dev, block, width)
        picked = jnp.take(blocks, source_block, axis=0)
        filled = jnp.where(occupied[:, None, None], picked, jnp.zeros((), rows_lo.dtype))
        outgoing = filled.reshape(experts, capacity * block, width)
        arrived = lax.all_to_all(outgoing, "expert", split_axis=0, concat_axis=0, tiled=True)
        return arrived.reshape(-1, width)

    def bring_home(partial_value):
        shaped = partial_value.reshape(experts, capacity * block, width)
        returned = lax.all_to_all(
            shaped.astype(jnp.bfloat16), "expert", split_axis=0, concat_axis=0, tiled=True
        ).astype(shaped.dtype)
        mine = jnp.take(returned.reshape(slot_total, block, width), slot_of_block, axis=0)
        result = lax.psum(mine.reshape(tok_rows, width).astype(jnp.bfloat16), "mp").astype(
            jnp.float32
        )
        return result

    up_matrix = weight_up[0]
    down_matrix = weight_down[0]
    contract_last = (((1,), (1,)), ((), ()))
    contract_first = (((0,), (0,)), ((), ()))
    routed_lo = dispatch(tokens.astype(jnp.bfloat16))
    pre_act = jnp.dot(routed_lo, up_matrix, preferred_element_type=jnp.float32)
    hidden = jax.nn.gelu(pre_act).astype(jnp.bfloat16)
    mixed_part = jnp.dot(hidden, down_matrix, preferred_element_type=jnp.float32)
    layer_output = tokens + bring_home(mixed_part)
    routed_up = dispatch(upstream.astype(jnp.bfloat16))
    hidden_grad = lax.dot_general(
        routed_up, down_matrix, contract_last, preferred_element_type=jnp.float32
    )
    unused, gelu_back = jax.vjp(jax.nn.gelu, pre_act)
    pre_grad = gelu_back(hidden_grad)[0].astype(jnp.bfloat16)
    token_part = lax.dot_general(
        pre_grad, up_matrix, contract_last, preferred_element_type=jnp.float32
    )
    up_part = lax.dot_general(
        routed_lo, pre_grad, contract_first, preferred_element_type=jnp.float32
    )
    down_part = lax.dot_general(
        hidden, routed_up, contract_first, preferred_element_type=jnp.float32
    )
    grad_tokens = upstream + bring_home(token_part)
    grad_up, grad_down = (
        lax.psum_scatter(
            up_part[None].astype(jnp.bfloat16), "dp", scatter_dimension=1, tiled=True
        ).astype(jnp.float32),
        lax.psum_scatter(
            down_part[None].astype(jnp.bfloat16), "dp", scatter_dimension=2, tiled=True
        ).astype(jnp.float32),
    )
    return (layer_output, grad_tokens, grad_up, grad_down)


def solution(mesh):
    placed = (
        P(("dp", "expert"), None),
        P(("dp", "expert"), None),
        P("expert", None, "mp"),
        P("expert", "mp", None),
        P(("dp", "expert"), None),
    )

    def body(tokens, block_experts, weight_up, weight_down, upstream):
        tok_rows, width = tokens.shape
        blocks_dev = block_experts.shape[0]
        fits = (
            (mesh.shape["dp"], mesh.shape["expert"], mesh.shape["mp"]) == (4, 4, 2)
            and blocks_dev % 2 == 0
            and (tok_rows // 4) % 16 == 0
            and width % (4 * TILE) == 0
            and weight_up.shape[2] % TILE == 0
        )
        chosen = fused_body if fits else plain_body
        return chosen(tokens, block_experts, weight_up, weight_down, upstream)

    return jax.shard_map(
        body,
        mesh=mesh,
        in_specs=placed,
        out_specs=(
            P(("dp", "expert"), None),
            P(("dp", "expert"), None),
            P("expert", "dp", "mp"),
            P("expert", "mp", "dp"),
        ),
        check_vma=False,
    )
```
